512 devices in a mesh: dp: 64 (over y, z), tower: 8 (over x, core).
Axes of the slice: x: 4, y: 8, z: 8, core: 2. Of those that a mesh axis runs over, the one named last changes fastest.
Arguments:
- rep: bfloat16 [16384, 2048], P('dp', 'tower'), may hold values from -6 to 6
- arm_ids: int32 [16384], P('dp'), may hold values from 0 to 63, as said below
- outcome: bfloat16 [16384], P('dp'), may hold values from -6 to 6
- weight: bfloat16 [16384], P('dp'), may hold values from 0.5 to 4
- w_hidden: bfloat16 [64, 2048, 2048], P('dp', None, 'tower'), may hold values from -0.125 to 0.125
- b_hidden: float32 [64, 2048], P('dp', 'tower'), may hold values from -3 to 3
- w_head: float32 [64, 2048], P('dp', 'tower'), may hold values from -0.125 to 0.125
- b_head: float32 [64], P('dp'), may hold values from -4 to 4
Outputs:
- grad_hidden: float32 [64, 2048, 2048], P('dp', None, 'tower')
- grad_hidden_bias: float32 [64, 2048], P('dp', 'tower')
- grad_head: float32 [64, 2048], P('dp', 'tower')
- grad_head_bias: float32 [64], P('dp')
- grad_rep: bfloat16 [16384, 2048], P('dp', 'tower')
- predicted: bfloat16 [16384], P('dp')
The draws below stay inside these ranges and needn't reach their ends.
Inputs may be any that keep to these rules, and one draw needn't show every extreme that they name: `arm_ids`: among the 256 rows of one index of dp at most 14 name one arm, and in every draw some index has an arm named exactly 14 times; over all 16384 rows at most 512 name one arm, and in every draw some arm is named exactly 512 times.
All inputs are finite; a program needn't handle non-finite values.
Results may differ from the reference program's by a relative error of at most 0.019.
Values may be sent and summed in bfloat16 or wider, within the bound.
No kernel may reach another device: no remote copies, remote signals or barrier semaphores. Data moves between devices by JAX's collectives and lax.ppermute only.
A program may use at most 64 MiB of HBM per device.

```python
import math
import jax
import jax.numpy as jnp
from jax import lax

H = 2048
ROW_DP = 256
ARMS = 64
ROWS = 16384
SHARE = 2
N_TOWER = 8


def capped_counts(key, bin_count, sum_target, cap_each):
    key_hot, key_pick = jax.random.split(key)
    hot_bin = jax.random.randint(key_hot, (), 0, bin_count)
    slot_bin = jnp.repeat(jnp.arange(bin_count, dtype=jnp.int32), cap_each)
    shuffled = slot_bin[jax.random.permutation(key_pick, bin_count * cap_each)]
    usable = (shuffled != hot_bin).astype(jnp.int32)
    chosen = usable * (jnp.cumsum(usable) <= sum_target - cap_each).astype(jnp.int32)
    arm_labels = jnp.arange(bin_count, dtype=jnp.int32)
    counts = jnp.sum(chosen[:, None] * (shuffled[:, None] == arm_labels[None, :]).astype(jnp.int32), axis=0)
    return (counts + cap_each * (arm_labels == hot_bin).astype(jnp.int32)).astype(jnp.int32)


def draw_arm_ids(key, part):
    key = jax.random.fold_in(key, 11)
    key_skew, key_base, key_rows = jax.random.split(key, 3)
    skewed = capped_counts(key_skew, ARMS, ARMS * SHARE, 3 * SHARE)
    spread = capped_counts(key_base, ARMS, ARMS * SHARE, 4 * SHARE)
    arm_labels = jnp.arange(ARMS, dtype=jnp.int32)
    positions = jnp.arange(ROW_DP, dtype=jnp.int32)

    def one_block(source, block_key):
        counts = skewed + spread[(arm_labels - source) % ARMS]
        row_ends = jnp.cumsum(counts)
        arm_of_row = jnp.sum((positions[:, None] >= row_ends[None, :]).astype(jnp.int32), axis=1)
        return arm_of_row[jax.random.permutation(block_key, ROW_DP)]
    blocks = jax.vmap(one_block)(arm_labels, jax.random.split(key_rows, ARMS))
    return blocks.reshape(ROWS).astype(jnp.int32)


def shard_levels(stream_key, shape, cuts, low, high):
    loudness, own = 1.0, jax.random.fold_in(stream_key, 6)
    for dim, parts in cuts:
        heights = jnp.exp(jax.random.uniform(jax.random.fold_in(own, dim), (parts,), jnp.float32, low / len(cuts), high / len(cuts)))
        loudness = loudness * jnp.repeat(heights, shape[dim] // parts).reshape([-1 if axis == dim else 1 for axis in range(len(shape))])
    return loudness


def centred(own_key, shape, scale, most, pieces=(), held_as=jnp.bfloat16):
    values = jax.random.normal(own_key, shape, jnp.float32) * scale
    if len(pieces) > 0:
        values = shard_levels(own_key, shape, pieces, -0.22, 0.18) * values
    return jnp.clip(values, min=-most, max=most).astype(held_as)


def setup_inputs(seed: int = 0) -> dict:
    seeds = jax.random.split(jax.random.key(seed), 9)
    rep = centred(seeds[0], (ROWS, H), 1.0, 6.0, ((0, 64), (1, 8)))
    arm_ids = draw_arm_ids(jax.random.fold_in(seeds[8], 71), 0)
    outcome = centred(seeds[2], (ROWS,), 1.0, 6.0, ((0, 64),))
    weight = jnp.clip(jnp.exp(math.log(4.0) - 2.0794415 * jax.random.uniform(seeds[3], (ROWS,), jnp.float32) ** shard_levels(seeds[3], (ROWS,), ((0, 64),), -0.2, 0.2)), 0.5, 4.0).astype(jnp.bfloat16)
    w_hidden = centred(seeds[4], (ARMS, H, H), H ** -0.5, 0.125, ((0, 64), (2, 8)))
    b_hidden = centred(seeds[5], (ARMS, H), 0.5, 3.0, ((0, 64), (1, 8)), jnp.float32)
    w_head = centred(seeds[6], (ARMS, H), H ** -0.5, 0.125, ((0, 64), (1, 8)), jnp.float32)
    b_head = centred(seeds[7], (ARMS,), 1.0, 4.0, ((0, 64),), jnp.float32)
    return {"rep": rep, "arm_ids": arm_ids, "outcome": outcome, "weight": weight, "w_hidden": w_hidden, "b_hidden": b_hidden, "w_head": w_head, "b_head": b_head}


def reference(rep, arm_ids, outcome, weight, w_hidden, b_hidden, w_head, b_head):
    total_rows = rep.shape[0]
    width = rep.shape[1]
    packed = 2 * ROW_DP
    block_width = width // N_TOWER
    order = jnp.argsort(arm_ids, stable=True).astype(jnp.int32)
    arm_labels = jnp.arange(ARMS, dtype=jnp.int32)
    counts = jnp.sum((arm_ids[:, None] == arm_labels[None, :]).astype(jnp.int32), axis=0).astype(jnp.int32)
    starts = (jnp.cumsum(counts) - counts).astype(jnp.int32)
    slot_index = jnp.arange(packed, dtype=jnp.int32)

    def one_arm(arm_index):
        live_slot = slot_index < counts[arm_index]
        where_rows = order[jnp.minimum(starts[arm_index] + slot_index, total_rows - 1)].astype(jnp.int32)
        inputs = rep[where_rows]
        weights = jnp.where(live_slot, weight[where_rows].astype(jnp.float32), jnp.float32(0.0))
        targets = outcome[where_rows].astype(jnp.float32)
        matrix = w_hidden[arm_index]
        head_cols = w_head[arm_index]
        pre_act = jnp.dot(inputs, matrix, preferred_element_type=jnp.float32) + b_hidden[arm_index]
        sigmoid_pre = jax.nn.sigmoid(pre_act)
        activation = pre_act * sigmoid_pre
        full_pred = jnp.sum(activation * head_cols, axis=1) + b_head[arm_index]
        resid_grad = weights * (full_pred - targets)
        pre_grad = resid_grad[:, None] * head_cols * sigmoid_pre * (1.0 + pre_act * (1.0 - sigmoid_pre))
        pre_grad_half = pre_grad.astype(jnp.bfloat16)
        grad_matrix = jnp.dot(inputs.T, pre_grad_half, preferred_element_type=jnp.float32)
        grad_bias = jnp.sum(pre_grad, axis=0)
        grad_vector = jnp.sum(resid_grad[:, None] * activation, axis=0)
        grad_scalar = jnp.sum(resid_grad)
        blocks = pre_grad_half.astype(jnp.float32).reshape(packed, N_TOWER, block_width)
        columns = matrix.astype(jnp.float32).reshape(width, N_TOWER, block_width)
        rep_part = jnp.einsum("skc,hkc->skh", blocks, columns).astype(jnp.bfloat16)
        grad_rows = jnp.sum(rep_part.astype(jnp.float32), axis=1).astype(jnp.bfloat16)
        row_target = jnp.where(live_slot, where_rows, total_rows).astype(jnp.int32)
        return grad_matrix, grad_bias, grad_vector, grad_scalar, grad_rows, full_pred.astype(jnp.bfloat16), row_target

    results = lax.map(one_arm, arm_labels)
    grad_hidden, grad_hidden_bias, grad_head, grad_head_bias, rows_all, pred_all, target_all = results
    flat_target = target_all.reshape(-1)
    grad_rep = jnp.zeros((total_rows, width), jnp.bfloat16).at[flat_target].set(rows_all.reshape(-1, width), mode="drop")
    predicted = jnp.zeros((total_rows,), jnp.bfloat16).at[flat_target].set(pred_all.reshape(-1), mode="drop")
    return grad_hidden, grad_hidden_bias, grad_head, grad_head_bias, grad_rep, predicted
```

```python
import functools

import jax
import jax.numpy as jnp
from jax import lax
from jax.experimental import pallas as pl
from jax.experimental.pallas import tpu as pltpu
from jax.sharding import PartitionSpec as P

F32, BF16, I32 = jnp.float32, jnp.bfloat16, jnp.int32
SLOT = 16
SIDE = 14
EXTRA = 16
INTERPRET = False

NN = (((1,), (0,)), ((), ()))
NT = (((1,), (1,)), ((), ()))
TN = (((0,), (0,)), ((), ()))


def mm(a, b, dims=NN):
    return lax.dot_general(a, b, dims, preferred_element_type=F32)


def iota(shape, dim):
    return lax.broadcasted_iota(I32, shape, dim)


def ones_where(mask):
    return jnp.where(mask, 1.0, 0.0).astype(BF16)


def call(kernel, out_shape, n_smem=0, flops=0, nbytes=0, vmem=32):
    def run(*args):
        specs = [pl.BlockSpec(memory_space=pltpu.SMEM)] * n_smem
        specs += [pl.BlockSpec(memory_space=pltpu.VMEM)] * (len(args) - n_smem)
        many = isinstance(out_shape, (tuple, list))
        out_spec = pl.BlockSpec(memory_space=pltpu.VMEM)
        return pl.pallas_call(
            kernel,
            out_shape=out_shape,
            in_specs=specs,
            out_specs=[out_spec] * len(out_shape) if many else out_spec,
            compiler_params=pltpu.CompilerParams(vmem_limit_bytes=vmem * 2**20),
            cost_estimate=pl.CostEstimate(flops=flops, bytes_accessed=nbytes, transcendentals=0),
            interpret=INTERPRET,
        )(*args)

    return run


def sds(shape, dtype):
    return jax.ShapeDtypeStruct(shape, dtype)


def side_rows(arms):
    shape = (arms * SLOT, arms)
    return ones_where(iota(shape, 0) == iota(shape, 1) * SLOT + SIDE)


def pick_side(arms):
    shape = (arms, arms * SLOT)
    return ones_where(iota(shape, 1) == iota(shape, 0) * SLOT + SIDE)


def pack_kernel(arms, arm_ref, outcome_ref, weight_ref, rep_ref, slots_ref, slot_ref, rank_ref):
    rows, width = rep_ref.shape
    ids = arm_ref[...]
    hot = iota((arms, rows), 0) == ids
    hot_half = ones_where(hot)
    earlier = ones_where(iota((rows, rows), 0) < iota((rows, rows), 1))
    counts = mm(hot_half, earlier)
    rank = jnp.sum(jnp.where(hot, counts, 0.0), axis=0, keepdims=True).astype(I32)
    slot = ids * SLOT + rank
    slot_ref[...] = slot
    rank_ref[...] = rank
    place = ones_where(iota((arms * SLOT, rows), 0) == slot)
    lane = iota((width, rows), 0)
    side_t = jnp.where(lane == rank, outcome_ref[...].astype(F32), 0.0) + jnp.where(
        lane == rank + SLOT, weight_ref[...].astype(F32), 0.0
    )
    side = mm(hot_half, side_t.astype(BF16), NT).astype(BF16)
    slots_ref[...] = (mm(place, rep_ref[...]) + mm(side_rows(arms), side)).astype(BF16)


def compact_kernel(arms, packed, slots_ref, rows_ref, side_ref, pos_ref):
    total, width = slots_ref.shape
    slots = slots_ref[...]
    side = mm(pick_side(arms), slots)
    lane8 = iota((8, width), 1)
    weight_lanes = ones_where((lane8 >= SLOT) & (lane8 < 2 * SLOT))
    counts = mm(weight_lanes, ones_where(side > 0.0), NT).astype(BF16)
    source, owner = iota((arms, total), 0), iota((arms, total), 1) // SLOT
    same = source == owner
    start = mm(counts, ones_where(source < owner))
    count = mm(counts, ones_where(same))
    depth = iota((8, total), 1) % SLOT
    pos = jnp.where(depth < count.astype(I32), start.astype(I32) + depth, 2 * packed)
    pos_ref[...] = pos
    gather = ones_where(iota((packed, total), 0) == pos[0:1])
    rows_ref[...] = mm(gather, slots).astype(BF16)
    side_half = side.astype(BF16)
    lane, place = iota((width, total), 0), iota((width, total), 1) % SLOT
    target = mm(side_half, ones_where(lane == place))
    weight = mm(side_half, ones_where(lane == place + SLOT))
    target = jnp.sum(jnp.where(same, target, 0.0), axis=0, keepdims=True)
    weight = jnp.sum(jnp.where(same, weight, 0.0), axis=0, keepdims=True)
    both = jnp.where(iota((8, total), 0) == 0, target, weight)
    side_ref[...] = mm(both.astype(BF16), gather, NT)


def split_pair(value):
    high = value.astype(BF16)
    return high, (value - high.astype(F32)).astype(BF16)


def forward_kernel(
    block_ref, x0, x1, x2, x3, y0, y1, y2, y3, w_ref, b_ref, head_ref,
    act_ref, g_ref, keep_ref, send_ref, share_ref,
):
    rows, width = x0.shape
    pre = jnp.zeros((rows, b_ref.shape[1]), F32)
    for j, x_ref in enumerate((x0, x1, x2, x3, y0, y1, y2, y3)):
        pre += mm(x_ref[...], w_ref[block_ref[j]])
    pre = pre + b_ref[...]
    sig = jax.nn.sigmoid(pre)
    head = head_ref[...]
    act = pre * sig
    g = head * sig * (1.0 + pre * (1.0 - sig))
    act_ref[...] = act
    g_ref[...] = g
    g_half = g.astype(BF16)
    share = lax.dot_general(
        jnp.broadcast_to(head, (8, head.shape[1])), act, NT,
        precision=lax.Precision.HIGHEST, preferred_element_type=F32,
    )
    for j in range(4):
        keep_ref[j] = mm(g_half, w_ref[block_ref[j]], NT).astype(BF16)
        send_ref[pl.ds(j * rows, rows), :] = mm(g_half, w_ref[block_ref[4 + j]], NT).astype(BF16)
    high, low = split_pair(share)
    share_ref[...] = high.astype(F32) + low.astype(F32)
    send_ref[pl.ds(4 * rows, EXTRA), :] = extra_rows(high, low, width)


def extra_rows(high, low, width):
    parts = high.shape[1] // width
    row = iota((EXTRA, width), 0)
    out = jnp.zeros((EXTRA, width), F32)
    for i in range(parts):
        piece = slice(i * width, (i + 1) * width)
        out = jnp.where(row == i, high[0:1, piece].astype(F32), out)
        out = jnp.where(row == parts + i, low[0:1, piece].astype(F32), out)
    return out.astype(BF16)


def read_extra(extra, parts):
    extra = extra.astype(F32)
    both = [extra[i : i + 1] + extra[parts + i : parts + i + 1] for i in range(parts)]
    return jnp.concatenate(both, axis=1)


def chip_sum_kernel(keep_ref, got_ref, share_ref, own_ref, m1_ref, m2_ref, m3_ref, chip_ref):
    _, rows, width = keep_ref.shape
    parts = rows // width
    share = share_ref[0:1] + read_extra(got_ref[pl.ds(4 * rows, EXTRA), :], parts)
    high, low = split_pair(share)
    chip_ref[...] = jnp.broadcast_to(high.astype(F32) + low.astype(F32), chip_ref.shape)
    extra = extra_rows(high, low, width)
    for j, out in enumerate((own_ref, m1_ref, m2_ref, m3_ref)):
        total = keep_ref[j].astype(F32) + got_ref[pl.ds(j * rows, rows), :].astype(F32)
        if j == 0:
            out[...] = total
        else:
            out[pl.ds(0, rows), :] = total.astype(BF16)
            out[pl.ds(rows, EXTRA), :] = extra


def back_kernel(arms, own_ref, r1_ref, r2_ref, r3_ref, chip_ref, side_ref, pos_ref, bias_ref, slots_ref, resid_ref):
    rows, width = own_ref.shape
    parts = rows // width
    total = arms * SLOT
    tail = pl.ds(rows, EXTRA)
    near = read_extra(r1_ref[tail, :], parts) + read_extra(r2_ref[tail, :], parts)
    pred = ((chip_ref[0:1] + read_extra(r3_ref[tail, :], parts)) + near) + bias_ref[0]
    resid = side_ref[1:2] * (pred - side_ref[0:1])
    resid_col = jnp.transpose(jnp.broadcast_to(resid, (128, rows)))
    resid_ref[...] = resid_col
    body = pl.ds(0, rows)
    grad = own_ref[...] + r1_ref[body, :].astype(F32) + r2_ref[body, :].astype(F32) + r3_ref[body, :].astype(F32)
    grad = (grad * resid_col[:, 0:1]).astype(BF16)
    gather = ones_where(iota((rows, total), 0) == pos_ref[0:1])
    pred_slot = mm(jnp.broadcast_to(pred, (8, rows)).astype(BF16), gather)
    same = iota((arms, total), 0) == iota((arms, total), 1) // SLOT
    spread = jnp.where(same, pred_slot[0:1], 0.0).astype(BF16)
    lane = ones_where(iota((width, total), 0) == iota((width, total), 1) % SLOT)
    pred_side = mm(spread, lane, NT).astype(BF16)
    slots_ref[...] = (mm(gather, grad, TN) + mm(side_rows(arms), pred_side)).astype(BF16)


def unpack_kernel(arms, slots_ref, slot_ref, rank_ref, arm_ref, grad_ref, pred_ref):
    total, width = slots_ref.shape
    rows = slot_ref.shape[1]
    slots = slots_ref[...]
    place = ones_where(iota((total, rows), 0) == slot_ref[...])
    grad_ref[...] = mm(place, slots, TN).astype(BF16)
    pred_side = mm(pick_side(arms), slots).astype(BF16)
    by_arm = mm(pred_side, ones_where(iota((width, rows), 0) == rank_ref[...]))
    hot = iota((arms, rows), 0) == arm_ref[...]
    pred_ref[...] = jnp.sum(jnp.where(hot, by_arm, 0.0), axis=0, keepdims=True).astype(BF16)


def grads_kernel(
    block_ref, x0, x1, x2, x3, y0, y1, y2, y3, act_ref, g_ref, resid_ref,
    matrix_ref, bias_ref, head_ref, scalar_ref,
):
    resid = resid_ref[...]
    resid_col = resid[:, 0:1]
    pre_grad = g_ref[...] * resid_col
    bias_ref[...] = jnp.sum(pre_grad, axis=0, keepdims=True)
    head_ref[...] = jnp.sum(act_ref[...] * resid_col, axis=0, keepdims=True)
    scalar_ref[...] = jnp.sum(resid, axis=0, keepdims=True)
    pre_half = pre_grad.astype(BF16)
    for j, x_ref in enumerate((x0, x1, x2, x3, y0, y1, y2, y3)):
        matrix_ref[block_ref[j]] = mm(x_ref[...], pre_half, TN)


def body(rep, arm_ids, outcome, weight, w_hidden, b_hidden, w_head, b_head):
    arms = lax.axis_size("dp")
    tower = lax.axis_size("tower")
    chips = tower // 2
    rows, width = rep.shape
    packed = 2 * rows
    total = arms * SLOT
    hidden = w_hidden.shape[2]

    t = lax.axis_index("tower")
    chip, core = t // 2, t % 2
    near = [(chip + d) % chips for d in (0, chips - 1, 1, 2)]
    block = jnp.stack([n * 2 + core for n in near] + [n * 2 + 1 - core for n in near]).astype(I32)

    def hop(value, by):
        return lax.ppermute(value, "tower", [(i, (i + 2 * by) % tower) for i in range(tower)])

    def swap(value):
        return lax.ppermute(value, "tower", [(i, i ^ 1) for i in range(tower)])

    def exchange(slots):
        cut = slots.reshape(arms, SLOT, width)
        return lax.all_to_all(cut, "dp", split_axis=0, concat_axis=0, tiled=True).reshape(total, width)

    ids = arm_ids.reshape(1, rows)
    slots, slot, rank = call(
        functools.partial(pack_kernel, arms),
        (sds((total, width), BF16), sds((1, rows), I32), sds((1, rows), I32)),
        flops=2 * total * rows * width,
    )(ids, outcome.reshape(1, rows), weight.reshape(1, rows), rep)
    arrived = exchange(slots)
    x0, side, pos = call(
        functools.partial(compact_kernel, arms, packed),
        (sds((packed, width), BF16), sds((8, packed), F32), sds((8, total), I32)),
        flops=2 * total * packed * width,
    )(arrived)
    x3, x1, x2 = hop(x0, 2), hop(x0, 1), hop(x0, -1)
    xs = (x0, x1, x2, x3)
    ys = tuple(swap(x) for x in xs)
    matrix = w_hidden.reshape(tower, width, hidden)
    act, g, keep, send, share = call(
        forward_kernel,
        (
            sds((packed, hidden), F32),
            sds((packed, hidden), F32),
            sds((chips, packed, width), BF16),
            sds((chips * packed + EXTRA, width), BF16),
            sds((8, packed), F32),
        ),
        n_smem=1,
        flops=4 * packed * tower * width * hidden,
    )(block, *xs, *ys, matrix, b_hidden, w_head)
    got = swap(send)
    own, m1, m2, m3, chip_share = call(
        chip_sum_kernel,
        (sds((packed, width), F32),)
        + (sds((packed + EXTRA, width), BF16),) * 3
        + (sds((8, packed), F32),),
    )(keep, got, share)
    r3, r1, r2 = hop(m3, 2), hop(m1, -1), hop(m2, 1)
    back_slots, resid = call(
        lambda bias, *refs: back_kernel(arms, *refs[:7], bias, *refs[7:]),
        (sds((total, width), BF16), sds((packed, 128), F32)),
        n_smem=1,
        flops=2 * total * packed * width,
    )(b_head, own, r1, r2, r3, chip_share, side, pos)
    returned = exchange(back_slots)
    grad_matrix, grad_bias, grad_vector, grad_scalar = call(
        grads_kernel,
        (
            sds((tower, width, hidden), F32),
            sds((1, hidden), F32),
            sds((1, hidden), F32),
            sds((1, 128), F32),
        ),
        n_smem=1,
        flops=2 * packed * tower * width * hidden,
        nbytes=5 * 2**20,
    )(block, *xs, *ys, act, g, resid)
    grad_rep, predicted = call(
        functools.partial(unpack_kernel, arms),
        (sds((rows, width), BF16), sds((1, rows), BF16)),
        flops=2 * total * rows * width,
    )(returned, slot, rank, ids)
    return (
        grad_matrix.reshape(1, tower * width, hidden),
        grad_bias,
        grad_vector,
        grad_scalar[0, :1],
        grad_rep,
        predicted.reshape(rows),
    )


def solution(mesh):
    return jax.shard_map(
        body,
        mesh=mesh,
        in_specs=(
            P("dp", "tower"),
            P("dp"),
            P("dp"),
            P("dp"),
            P("dp", None, "tower"),
            P("dp", "tower"),
            P("dp", "tower"),
            P("dp"),
        ),
        out_specs=(
            P("dp", None, "tower"),
            P("dp", "tower"),
            P("dp", "tower"),
            P("dp"),
            P("dp", "tower"),
            P("dp"),
        ),
        check_vma=False,
    )
```

```python
import functools

import jax
import jax.numpy as jnp
from jax import lax
from jax.experimental import pallas as pl
from jax.experimental.pallas import tpu as pltpu
from jax.sharding import PartitionSpec as P

F32, BF16, I32 = jnp.float32, jnp.bfloat16, jnp.int32
SLOT = 16
SIDE = 14
EXTRA = 16
INTERPRET = False
VMEM, SMEM, ANY = pltpu.VMEM, pltpu.SMEM, pl.ANY

NN = (((1,), (0,)), ((), ()))
NT = (((1,), (1,)), ((), ()))
TN = (((0,), (0,)), ((), ()))


def mm(a, b, dims=NN):
    return lax.dot_general(a, b, dims, preferred_element_type=F32)


def iota(shape, dim):
    return lax.broadcasted_iota(I32, shape, dim)


def ones_where(mask):
    return jnp.where(mask, 1.0, 0.0).astype(BF16)


def call(kernel, out_shape, spaces=None, outs=None, scratch=(), flops=0, nbytes=0, vmem=32):
    def run(*args):
        return pl.pallas_call(
            kernel,
            out_shape=out_shape,
            in_specs=[pl.BlockSpec(memory_space=m) for m in spaces or [VMEM] * len(args)],
            out_specs=[pl.BlockSpec(memory_space=m) for m in outs or [VMEM] * len(out_shape)],
            scratch_shapes=list(scratch),
            compiler_params=pltpu.CompilerParams(vmem_limit_bytes=vmem * 2**20),
            cost_estimate=pl.CostEstimate(flops=flops, bytes_accessed=nbytes, transcendentals=0),
            interpret=INTERPRET,
        )(*args)

    return run


def sds(shape, dtype):
    return jax.ShapeDtypeStruct(shape, dtype)


def side_rows(arms):
    shape = (arms * SLOT, arms)
    return ones_where(iota(shape, 0) == iota(shape, 1) * SLOT + SIDE)


def pick_side(arms):
    shape = (arms, arms * SLOT)
    return ones_where(iota(shape, 1) == iota(shape, 0) * SLOT + SIDE)


def pack_kernel(arms, meta_ref, rep_hbm, slots_ref, aux_ref, rep_ref, sem):
    copy = pltpu.make_async_copy(rep_hbm, rep_ref, sem)
    copy.start()
    rows, width = rep_ref.shape
    ids = meta_ref[0:1].astype(I32)
    hot = iota((arms, rows), 0) == ids
    hot_half = ones_where(hot)
    earlier = ones_where(iota((rows, rows), 0) < iota((rows, rows), 1))
    counts = mm(hot_half, earlier)
    rank = jnp.sum(jnp.where(hot, counts, 0.0), axis=0, keepdims=True).astype(I32)
    slot = ids * SLOT + rank
    row8 = iota((8, rows), 0)
    aux_ref[...] = jnp.where(row8 == 0, slot, jnp.where(row8 == 1, rank, ids))
    place = ones_where(iota((arms * SLOT, rows), 0) == slot)
    lane = iota((width, rows), 0)
    side_t = jnp.where(lane == rank, meta_ref[1:2], 0.0) + jnp.where(lane == rank + SLOT, meta_ref[2:3], 0.0)
    side = mm(hot_half, side_t.astype(BF16), NT).astype(BF16)
    side_part = mm(side_rows(arms), side)
    copy.wait()
    slots_ref[...] = (mm(place, rep_ref[...]) + side_part).astype(BF16)


def compact_kernel(arms, packed, slots_ref, send_ref, side_ref, pos_ref):
    total, width = slots_ref.shape
    slots = slots_ref[...]
    side = mm(pick_side(arms), slots)
    lane8 = iota((8, width), 1)
    weight_lanes = ones_where((lane8 >= SLOT) & (lane8 < 2 * SLOT))
    counts = mm(weight_lanes, ones_where(side > 0.0), NT).astype(BF16)
    source, owner = iota((arms, total), 0), iota((arms, total), 1) // SLOT
    same = source == owner
    start = mm(counts, ones_where(source < owner))
    count = mm(counts, ones_where(same))
    depth = iota((8, total), 1) % SLOT
    pos = jnp.where(depth < count.astype(I32), start.astype(I32) + depth, 2 * packed)
    pos_ref[...] = pos
    gather = ones_where(iota((packed, total), 0) == pos[0:1])
    rows = mm(gather, slots).astype(BF16)
    half = packed // 2
    for d in range(send_ref.shape[0]):
        send_ref[d] = rows[(d % 2) * half : (d % 2 + 1) * half]
    side_half = side.astype(BF16)
    lane, place = iota((width, total), 0), iota((width, total), 1) % SLOT
    target = mm(side_half, ones_where(lane == place))
    weight = mm(side_half, ones_where(lane == place + SLOT))
    target = jnp.sum(jnp.where(same, target, 0.0), axis=0, keepdims=True)
    weight = jnp.sum(jnp.where(same, weight, 0.0), axis=0, keepdims=True)
    both = jnp.where(iota((8, total), 0) == 0, target, weight)
    side_ref[...] = mm(both.astype(BF16), gather, NT)


def column(row):
    return jnp.transpose(jnp.broadcast_to(row, (128, row.shape[1])))


def half_unit(x_ref, w_ref, bias, head):
    pre = jnp.broadcast_to(bias, (x_ref.shape[1], bias.shape[1]))
    for j in range(x_ref.shape[0]):
        pre += mm(x_ref[j], w_ref[j])
    sig = jax.nn.sigmoid(pre)
    return pre * sig, head * sig * (1.0 + pre * (1.0 - sig))


def forward_kernel(x_ref, near_ref, far_ref, bh_ref, far_bh_ref, msg_ref, over_ref, act_ref, g_ref):
    blocks, rows, width = x_ref.shape
    head, far_head = bh_ref[1:2], far_bh_ref[1:2]
    act, g = half_unit(x_ref, near_ref, bh_ref[0:1], head)
    far_act, far_g = half_unit(x_ref, far_ref, far_bh_ref[0:1], far_head)
    act_ref[...] = act
    g_ref[...] = g
    g, far_g = g.astype(BF16), far_g.astype(BF16)
    over_ref[0] = far_act.astype(BF16)
    over_ref[1] = far_g
    share = act * head + far_act * far_head
    cut = min(128, width)
    share = sum(share[:, i : i + cut] for i in range(0, width, cut))
    share = jnp.sum(jnp.transpose(share), axis=0, keepdims=True)
    high = share.astype(BF16).astype(F32)
    row = iota((EXTRA, rows), 0)
    extra = jnp.where(row == 0, high, jnp.where(row == 1, share - high, 0.0)).astype(BF16)
    for j in range(blocks):
        part = mm(g, near_ref[j], NT) + mm(far_g, far_ref[j], NT)
        msg_ref[j, pl.ds(0, rows), :] = part.astype(BF16)
        msg_ref[j, pl.ds(rows, EXTRA), pl.ds(0, rows)] = extra


def back_kernel(arms, bias_ref, got_ref, side_ref, pos_ref, slots_ref, resid_ref):
    blocks, rows, width = got_ref.shape
    rows = rows - EXTRA
    total = arms * SLOT
    preds, grads = [], []
    for half in range(2):
        extra = sum(got_ref[j, pl.ds(rows, EXTRA), pl.ds(0, rows)].astype(F32) for j in range(half, blocks, 2))
        preds.append(extra[0:1] + extra[1:2])
        grads.append(sum(got_ref[j, pl.ds(0, rows), :].astype(F32) for j in range(half, blocks, 2)))
    pred = jnp.concatenate(preds, axis=1) + bias_ref[0]
    resid = side_ref[1:2] * (pred - side_ref[0:1])
    resid_ref[...] = jnp.broadcast_to(resid, resid_ref.shape)
    grad = (jnp.concatenate(grads, axis=0) * column(resid)[:, 0:1]).astype(BF16)
    gather = ones_where(iota((2 * rows, total), 0) == pos_ref[0:1])
    pred_slot = mm(jnp.broadcast_to(pred, (8, 2 * rows)).astype(BF16), gather)
    same = iota((arms, total), 0) == iota((arms, total), 1) // SLOT
    spread = jnp.where(same, pred_slot[0:1], 0.0).astype(BF16)
    lane = ones_where(iota((width, total), 0) == iota((width, total), 1) % SLOT)
    pred_side = mm(spread, lane, NT).astype(BF16)
    slots_ref[...] = (mm(gather, grad, TN) + mm(side_rows(arms), pred_side)).astype(BF16)


def unpack_kernel(arms, slots_ref, aux_ref, grad_ref, pred_ref):
    total, width = slots_ref.shape
    rows = aux_ref.shape[1]
    slots = slots_ref[...]
    place = ones_where(iota((total, rows), 0) == aux_ref[0:1])
    grad_ref[...] = mm(place, slots, TN).astype(BF16)
    pred_side = mm(pick_side(arms), slots).astype(BF16)
    by_arm = mm(pred_side, ones_where(iota((width, rows), 0) == aux_ref[1:2]))
    hot = iota((arms, rows), 0) == aux_ref[2:3]
    pred_ref[...] = jnp.sum(jnp.where(hot, by_arm, 0.0), axis=0, keepdims=True).astype(BF16)


def grads_kernel(
    core_ref, x_ref, far_x_ref, act_ref, g_ref, over_ref, resid_ref, matrix_ref, bias_ref, head_ref, scalar_ref
):
    first = core_ref[0] == 0
    half = act_ref.shape[0]
    low, high = resid_ref[0:1, 0:half], resid_ref[0:1, half : 2 * half]
    scalar_ref[0] = jnp.sum(resid_ref[0:1])
    mine = column(jnp.where(first, low, high))[:, 0:1]
    other = column(jnp.where(first, high, low))[:, 0:1]
    near, far = g_ref[...] * mine, over_ref[1].astype(F32) * other
    bias_ref[...] = jnp.sum(near, axis=0, keepdims=True) + jnp.sum(far, axis=0, keepdims=True)
    head_ref[...] = jnp.sum(act_ref[...] * mine, axis=0, keepdims=True) + jnp.sum(
        over_ref[0].astype(F32) * other, axis=0, keepdims=True
    )
    near, far = near.astype(BF16), far.astype(BF16)
    for j in range(x_ref.shape[0]):
        matrix_ref[j] = mm(x_ref[j], near, TN) + mm(far_x_ref[j], far, TN)


def body(rep, arm_ids, outcome, weight, w_hidden, b_hidden, w_head, b_head):
    arms = lax.axis_size("dp")
    tower = lax.axis_size("tower")
    rows, width = rep.shape
    packed = 2 * rows
    total = arms * SLOT
    hidden = w_hidden.shape[2]
    core = (lax.axis_index("tower") % 2).astype(I32).reshape(1)

    def swap(value):
        return lax.ppermute(value, "tower", [(i, i ^ 1) for i in range(tower)])

    def exchange(slots):
        cut = slots.reshape(arms, SLOT, width)
        return lax.all_to_all(cut, "dp", split_axis=0, concat_axis=0, tiled=True).reshape(total, width)

    def spread(blocks):
        return lax.all_to_all(blocks, "tower", split_axis=0, concat_axis=0, tiled=True)

    meta = jnp.stack([arm_ids.astype(F32), outcome.astype(F32), weight.astype(F32)])
    slots, aux = call(
        functools.partial(pack_kernel, arms),
        (sds((total, width), BF16), sds((8, rows), I32)),
        spaces=[VMEM, ANY],
        scratch=[pltpu.VMEM((rows, width), BF16), pltpu.SemaphoreType.DMA],
        flops=2 * total * rows * width,
    )(meta, rep)
    arrived = exchange(slots)
    send, side, pos = call(
        functools.partial(compact_kernel, arms, packed),
        (sds((tower, rows, width), BF16), sds((8, packed), F32), sds((8, total), I32)),
        flops=2 * total * packed * width,
    )(arrived)
    matrix = w_hidden.reshape(tower, width, hidden)
    both = jnp.concatenate([b_hidden, w_head], axis=0)
    inputs = spread(send)
    far_matrix, far_both = swap(matrix), swap(both)
    msg, over, act, g = call(
        forward_kernel,
        (
            sds((tower, rows + EXTRA, width), BF16),
            sds((2, rows, hidden), BF16),
            sds((rows, hidden), F32),
            sds((rows, hidden), F32),
        ),
        flops=8 * rows * tower * width * hidden,
    )(inputs, matrix, far_matrix, both, far_both)
    got = spread(msg)
    msg, inputs2, over = lax.optimization_barrier((msg, inputs, over))
    far_inputs, far_over = swap(inputs2), swap(over)
    back_slots, resid = call(
        functools.partial(back_kernel, arms),
        (sds((total, width), BF16), sds((8, packed), F32)),
        spaces=[SMEM, VMEM, VMEM, VMEM],
        flops=2 * total * packed * width,
    )(b_head, got, side, pos)
    returned = exchange(back_slots)
    grad_matrix, grad_bias, grad_vector, grad_scalar = call(
        grads_kernel,
        (
            sds((tower, width, hidden), F32),
            sds((1, hidden), F32),
            sds((1, hidden), F32),
            sds((1,), F32),
        ),
        spaces=[SMEM] + [VMEM] * 6,
        outs=[VMEM, VMEM, VMEM, SMEM],
        flops=2 * packed * tower * width * hidden,
        nbytes=5 * 2**20,
    )(core, inputs, far_inputs, act, g, far_over, resid)
    grad_rep, predicted = call(
        functools.partial(unpack_kernel, arms),
        (sds((rows, width), BF16), sds((1, rows), BF16)),
        flops=2 * total * rows * width,
    )(returned, aux)
    return (
        grad_matrix.reshape(1, tower * width, hidden),
        grad_bias,
        grad_vector,
        grad_scalar,
        grad_rep,
        predicted.reshape(rows),
    )


def solution(mesh):
    return jax.shard_map(
        body,
        mesh=mesh,
        in_specs=(
            P("dp", "tower"),
            P("dp"),
            P("dp"),
            P("dp"),
            P("dp", None, "tower"),
            P("dp", "tower"),
            P("dp", "tower"),
            P("dp"),
        ),
        out_specs=(
            P("dp", None, "tower"),
            P("dp", "tower"),
            P("dp", "tower"),
            P("dp"),
            P("dp", "tower"),
            P("dp"),
        ),
        check_vma=False,
    )
```

```python
import functools

import jax
import jax.numpy as jnp
from jax import lax
from jax.experimental import pallas as pl
from jax.experimental.pallas import tpu as pltpu
from jax.sharding import PartitionSpec as P

F32, BF16, I32 = jnp.float32, jnp.bfloat16, jnp.int32
SLOT = 16
SIDE = 14
EXTRA = 16
INTERPRET = False
VMEM, SMEM, HBM = pltpu.VMEM, pltpu.SMEM, pltpu.HBM
DMA = pltpu.SemaphoreType.DMA
LANES = 128
PARTS = 4

NN = (((1,), (0,)), ((), ()))
NT = (((1,), (1,)), ((), ()))
TN = (((0,), (0,)), ((), ()))


def mm(a, b, dims=NN):
    return lax.dot_general(a, b, dims, preferred_element_type=F32)


def iota(shape, dim):
    return lax.broadcasted_iota(I32, shape, dim)


def ones_where(mask):
    return jnp.where(mask, 1.0, 0.0).astype(BF16)


def call(kernel, out_shape, ins=None, outs=None, scratch=(), flops=0, nbytes=0, vmem=32):
    kinds = outs or [VMEM] * len(out_shape)

    def run(*args):
        spaces = ins or [VMEM] * len(args)
        args = [pltpu.with_memory_space_constraint(a, HBM) if m is HBM else a for a, m in zip(args, spaces)]
        return pl.pallas_call(
            kernel,
            out_shape=[HBM(o.shape, o.dtype) if m is HBM else o for o, m in zip(out_shape, kinds)],
            in_specs=[pl.BlockSpec(memory_space=m) for m in spaces],
            out_specs=[pl.BlockSpec(memory_space=m) for m in kinds],
            scratch_shapes=list(scratch),
            compiler_params=pltpu.CompilerParams(vmem_limit_bytes=vmem * 2**20),
            cost_estimate=pl.CostEstimate(flops=flops, bytes_accessed=nbytes, transcendentals=0),
            interpret=INTERPRET,
        )(*args)

    return run


def sds(shape, dtype):
    return jax.ShapeDtypeStruct(shape, dtype)


def pick_side(arms):
    shape = (arms, arms * SLOT)
    return ones_where(iota(shape, 1) == iota(shape, 0) * SLOT + SIDE)


def column(row):
    return jnp.transpose(jnp.broadcast_to(row, (LANES, row.shape[1])))


def pack_kernel(
    arms, ids_hbm, outcome_hbm, weight_hbm, rep_hbm, slots_hbm, aux_ref,
    ids_ref, outcome_ref, weight_ref, rep_ref, slots_ref, in_sem, out_sem,
):
    pairs = ((ids_hbm, ids_ref), (outcome_hbm, outcome_ref), (weight_hbm, weight_ref), (rep_hbm, rep_ref))
    loads = [pltpu.make_async_copy(a, b, in_sem.at[i]) for i, (a, b) in enumerate(pairs)]
    for load in loads:
        load.start()
    rows, width = rep_ref.shape
    earlier = ones_where(iota((rows, rows), 0) < iota((rows, rows), 1))
    loads[0].wait()
    ids = ids_ref[...]
    hot = iota((arms, rows), 0) == ids
    hot_half = ones_where(hot)
    counts = mm(hot_half, earlier)
    rank = jnp.sum(jnp.where(hot, counts, 0.0), axis=0, keepdims=True).astype(I32)
    slot = ids * SLOT + rank
    row8 = iota((8, rows), 0)
    aux_ref[...] = jnp.where(row8 == 0, slot, jnp.where(row8 == 1, rank, ids))
    lane = iota((width, rows), 0)
    loads[1].wait()
    loads[2].wait()
    outcome = outcome_ref[...].astype(F32).reshape(1, rows)
    weight = weight_ref[...].astype(F32).reshape(1, rows)
    side_t = jnp.where(lane == rank, outcome, 0.0) + jnp.where(lane == rank + SLOT, weight, 0.0)
    side = mm(hot_half, side_t.astype(BF16), NT).astype(BF16)
    loads[3].wait()
    rep = rep_ref[...]
    stores = []
    part = arms * SLOT // PARTS
    for i in range(PARTS):
        place = ones_where(iota((part, rows), 0) + i * part == slot)
        mark = ones_where(iota((part, arms), 0) + i * part == iota((part, arms), 1) * SLOT + SIDE)
        cut = pl.ds(i * part, part)
        slots_ref[cut, :] = (mm(place, rep) + mm(mark, side)).astype(BF16)
        stores.append(pltpu.make_async_copy(slots_ref.at[cut], slots_hbm.at[cut], out_sem.at[i]))
        stores[-1].start()
    for store in stores:
        store.wait()


def side_of(slots, arms):
    return mm(pick_side(arms), slots)


def compact_kernel(arms, packed, slots_ref, send_hbm, pos_ref, side_ref, rows_ref, sem):
    total, width = slots_ref.shape
    slots = slots_ref[...]
    side = side_of(slots, arms)
    side_ref[...] = side.astype(BF16)
    lane8 = iota((8, width), 1)
    weight_lanes = ones_where((lane8 >= SLOT) & (lane8 < 2 * SLOT))
    counts = mm(weight_lanes, ones_where(side > 0.0), NT).astype(BF16)
    source, owner = iota((arms, total), 0), iota((arms, total), 1) // SLOT
    start = mm(counts, ones_where(source < owner))
    count = mm(counts, ones_where(source == owner))
    depth = iota((8, total), 1) % SLOT
    pos = jnp.where(depth < count.astype(I32), start.astype(I32) + depth, 2 * packed)
    pos_ref[...] = pos
    half = packed // 2
    blocks = send_hbm.shape[0]
    stores = []
    for h in range(2):
        gather = ones_where(iota((half, total), 0) + h * half == pos[0:1])
        rows_ref[h] = mm(gather, slots).astype(BF16)
        for d in range(h, blocks, 2):
            stores.append(pltpu.make_async_copy(rows_ref.at[h], send_hbm.at[d], sem.at[d]))
            stores[-1].start()
    for store in stores:
        store.wait()


def prepare_kernel(arms, packed, given_ref, pos_ref, side_ref):
    total, width = arms * SLOT, given_ref.shape[1]
    side = given_ref[...]
    gather = ones_where(iota((packed, total), 0) == pos_ref[0:1])
    same = iota((arms, total), 0) == iota((arms, total), 1) // SLOT
    lane, place = iota((width, total), 0), iota((width, total), 1) % SLOT
    target = mm(side, ones_where(lane == place))
    weight = mm(side, ones_where(lane == place + SLOT))
    target = jnp.sum(jnp.where(same, target, 0.0), axis=0, keepdims=True)
    weight = jnp.sum(jnp.where(same, weight, 0.0), axis=0, keepdims=True)
    both = jnp.where(iota((8, total), 0) == 0, target, weight)
    side_ref[...] = mm(both.astype(BF16), gather, NT)


def unit(pre, head):
    sig = jax.nn.sigmoid(pre)
    return pre * sig, head * sig * (1.0 + pre * (1.0 - sig))


def forward_kernel(
    x_ref, near_ref, far_hbm, bh_ref, far_bh_ref, msg_hbm, over_hbm, act_hbm, g_hbm,
    far_ref, msg_ref, over_ref, act_ref, g_ref, in_sem, msg_sem, out_sem,
):
    blocks, rows, width = x_ref.shape
    loads = [pltpu.make_async_copy(far_hbm.at[j], far_ref.at[j], in_sem.at[j]) for j in range(blocks)]
    for load in loads:
        load.start()
    head, far_head = bh_ref[1:2], far_bh_ref[1:2]
    pre = sum(mm(x_ref[j], near_ref[j]) for j in range(blocks)) + bh_ref[0:1]
    act, g = unit(pre, head)
    act_ref[...] = act
    g_ref[...] = g
    g = g.astype(BF16)
    pre = jnp.broadcast_to(far_bh_ref[0:1], pre.shape)
    for j in range(blocks):
        loads[j].wait()
        pre += mm(x_ref[j], far_ref[j])
    far_act, far_g = unit(pre, far_head)
    far_g = far_g.astype(BF16)
    over_ref[0] = far_act.astype(BF16)
    over_ref[1] = far_g
    stores = [
        pltpu.make_async_copy(a, b, out_sem.at[i])
        for i, (a, b) in enumerate(((act_ref, act_hbm), (g_ref, g_hbm), (over_ref, over_hbm)))
    ]
    share = act * head + far_act * far_head
    cut = min(LANES, width)
    share = sum(share[:, i : i + cut] for i in range(0, width, cut))
    share = jnp.sum(jnp.transpose(share), axis=0, keepdims=True)
    high = share.astype(BF16).astype(F32)
    row = iota((EXTRA, rows), 0)
    extra = jnp.where(row == 0, high, jnp.where(row == 1, share - high, 0.0)).astype(BF16)
    for j in range(blocks):
        part = mm(g, near_ref[j], NT) + mm(far_g, far_ref[j], NT)
        msg_ref[j, pl.ds(0, rows), :] = part.astype(BF16)
        msg_ref[j, pl.ds(rows, EXTRA), pl.ds(0, rows)] = extra
        stores.append(pltpu.make_async_copy(msg_ref.at[j], msg_hbm.at[j], msg_sem.at[j]))
        stores[-1].start()
    for store in stores[:3]:
        store.start()
    for store in stores:
        store.wait()


def back_kernel(arms, bias_ref, got_ref, side_ref, pos_ref, slots_hbm, resid_ref, slots_ref, sem):
    blocks, rows, width = got_ref.shape
    rows = rows - EXTRA
    total = arms * SLOT
    preds, grads = [], []
    for half in range(2):
        extra = sum(got_ref[j, pl.ds(rows, EXTRA), pl.ds(0, rows)].astype(F32) for j in range(half, blocks, 2))
        preds.append(extra[0:1] + extra[1:2])
        grads.append(sum(got_ref[j, pl.ds(0, rows), :].astype(F32) for j in range(half, blocks, 2)))
    pred = jnp.concatenate(preds, axis=1) + bias_ref[0]
    resid = side_ref[1:2] * (pred - side_ref[0:1])
    resid_ref[...] = jnp.broadcast_to(resid, resid_ref.shape)
    grad = (jnp.concatenate(grads, axis=0) * column(resid)[:, 0:1]).astype(BF16)
    pred = jnp.broadcast_to(pred, (8, 2 * rows)).astype(BF16)
    stores = []
    part = total // PARTS
    for i in range(PARTS):
        cut = pl.ds(i * part, part)
        gather = ones_where(iota((2 * rows, part), 0) == pos_ref[0:1, i * part : (i + 1) * part])
        pred_slot = mm(pred, gather)[0:1]
        row, slot = iota((part, part), 0), iota((part, part), 1)
        spread = jnp.where((row % SLOT == SIDE) & (row // SLOT == slot // SLOT), pred_slot, 0.0).astype(BF16)
        lane = ones_where(iota((width, part), 0) == iota((width, part), 1) % SLOT)
        slots_ref[cut, :] = (mm(gather, grad, TN) + mm(spread, lane, NT)).astype(BF16)
        stores.append(pltpu.make_async_copy(slots_ref.at[cut], slots_hbm.at[cut], sem.at[i]))
        stores[-1].start()
    for store in stores:
        store.wait()


def unpack_kernel(arms, slots_ref, aux_ref, grad_ref, pred_ref):
    total, width = slots_ref.shape
    rows = aux_ref.shape[1]
    slots = slots_ref[...]
    place = ones_where(iota((total, rows), 0) == aux_ref[0:1])
    grad_ref[...] = mm(place, slots, TN).astype(BF16)
    pred_side = side_of(slots, arms).astype(BF16)
    by_arm = mm(pred_side, ones_where(iota((width, rows), 0) == aux_ref[1:2]))
    hot = iota((arms, rows), 0) == aux_ref[2:3]
    pred = jnp.sum(jnp.where(hot, by_arm, 0.0), axis=0, keepdims=True)
    pred_ref[...] = pred.reshape(rows).astype(BF16)


def grads_kernel(
    core_ref, x_ref, far_x_ref, act_ref, g_ref, over_ref, resid_ref, matrix_ref, bias_ref, head_ref, scalar_ref
):
    first = core_ref[0] == 0
    half = act_ref.shape[0]
    low, high = resid_ref[0:1, 0:half], resid_ref[0:1, half : 2 * half]
    scalar_ref[0] = jnp.sum(resid_ref[0:1])
    mine = column(jnp.where(first, low, high))[:, 0:1]
    other = column(jnp.where(first, high, low))[:, 0:1]
    near, far = g_ref[...] * mine, over_ref[1].astype(F32) * other
    bias_ref[...] = jnp.sum(near, axis=0, keepdims=True) + jnp.sum(far, axis=0, keepdims=True)
    head_ref[...] = jnp.sum(act_ref[...] * mine, axis=0, keepdims=True) + jnp.sum(
        over_ref[0].astype(F32) * other, axis=0, keepdims=True
    )
    near, far = near.astype(BF16), far.astype(BF16)
    for j in range(x_ref.shape[0]):
        matrix_ref[j] = mm(x_ref[j], near, TN) + mm(far_x_ref[j], far, TN)


def body(rep, arm_ids, outcome, weight, w_hidden, b_hidden, w_head, b_head):
    arms = lax.axis_size("dp")
    tower = lax.axis_size("tower")
    rows, width = rep.shape
    packed = 2 * rows
    total = arms * SLOT
    hidden = w_hidden.shape[2]
    core = (lax.axis_index("tower") % 2).astype(I32).reshape(1)

    def swap(value):
        return lax.ppermute(value, "tower", [(i, i ^ 1) for i in range(tower)])

    def exchange(slots):
        cut = slots.reshape(arms, SLOT, width)
        return lax.all_to_all(cut, "dp", split_axis=0, concat_axis=0, tiled=True).reshape(total, width)

    def spread(blocks):
        return lax.all_to_all(blocks, "tower", split_axis=0, concat_axis=0, tiled=True)

    slots, aux = call(
        functools.partial(pack_kernel, arms),
        (sds((total, width), BF16), sds((8, rows), I32)),
        ins=[HBM] * 4,
        outs=[HBM, VMEM],
        scratch=[
            VMEM((1, rows), I32), VMEM((rows,), BF16), VMEM((rows,), BF16), VMEM((rows, width), BF16),
            VMEM((total, width), BF16), DMA((4,)), DMA((PARTS,)),
        ],
        flops=2 * total * rows * width,
    )(arm_ids.reshape(1, rows), outcome, weight, rep)
    arrived = exchange(slots)
    send, pos, given = call(
        functools.partial(compact_kernel, arms, packed),
        (sds((tower, rows, width), BF16), sds((8, total), I32), sds((arms, width), BF16)),
        outs=[HBM, VMEM, VMEM],
        scratch=[VMEM((2, rows, width), BF16), DMA((tower,))],
        flops=2 * total * packed * width,
    )(arrived)
    matrix = w_hidden.reshape(tower, width, hidden)
    both = jnp.concatenate([b_hidden, w_head], axis=0)
    inputs = spread(send)
    far_matrix, far_both = swap(matrix), swap(both)
    (side,) = call(
        functools.partial(prepare_kernel, arms, packed),
        (sds((8, packed), F32),),
        flops=4 * total * packed * arms,
    )(given, pos)
    msg, over, act, g = call(
        forward_kernel,
        (
            sds((tower, rows + EXTRA, width), BF16),
            sds((2, rows, hidden), BF16),
            sds((rows, hidden), F32),
            sds((rows, hidden), F32),
        ),
        ins=[VMEM, VMEM, HBM, VMEM, VMEM],
        outs=[HBM] * 4,
        scratch=[
            VMEM((tower, width, hidden), BF16), VMEM((tower, rows + EXTRA, width), BF16),
            VMEM((2, rows, hidden), BF16), VMEM((rows, hidden), F32), VMEM((rows, hidden), F32),
            DMA((tower,)), DMA((tower,)), DMA((3,)),
        ],
        flops=8 * rows * tower * width * hidden,
    )(inputs, matrix, far_matrix, both, far_both)
    got = spread(msg)
    msg, inputs2, over = lax.optimization_barrier((msg, inputs, over))
    far_inputs, far_over = swap(inputs2), swap(over)
    back_slots, resid = call(
        functools.partial(back_kernel, arms),
        (sds((total, width), BF16), sds((8, packed), F32)),
        ins=[SMEM, VMEM, VMEM, VMEM],
        outs=[HBM, VMEM],
        scratch=[VMEM((total, width), BF16), DMA((PARTS,))],
        flops=2 * total * packed * width,
    )(b_head, got, side, pos)
    returned = exchange(back_slots)
    grad_matrix, grad_bias, grad_vector, grad_scalar = call(
        grads_kernel,
        (
            sds((tower, width, hidden), F32),
            sds((1, hidden), F32),
            sds((1, hidden), F32),
            sds((1,), F32),
        ),
        ins=[SMEM] + [VMEM] * 6,
        outs=[VMEM, VMEM, VMEM, SMEM],
        flops=2 * packed * tower * width * hidden,
        nbytes=5 * 2**20,
    )(core, inputs, far_inputs, act, g, far_over, resid)
    grad_rep, predicted = call(
        functools.partial(unpack_kernel, arms),
        (sds((rows, width), BF16), sds((rows,), BF16)),
        flops=2 * total * rows * width,
    )(returned, aux)
    return (
        grad_matrix.reshape(1, tower * width, hidden),
        grad_bias,
        grad_vector,
        grad_scalar,
        grad_rep,
        predicted,
    )


def solution(mesh):
    return jax.shard_map(
        body,
        mesh=mesh,
        in_specs=(
            P("dp", "tower"),
            P("dp"),
            P("dp"),
            P("dp"),
            P("dp", None, "tower"),
            P("dp", "tower"),
            P("dp", "tower"),
            P("dp"),
        ),
        out_specs=(
            P("dp", None, "tower"),
            P("dp", "tower"),
            P("dp", "tower"),
            P("dp"),
            P("dp", "tower"),
            P("dp"),
        ),
        check_vma=False,
    )
```

```python
import functools

import jax
import jax.numpy as jnp
from jax import lax
from jax.experimental import pallas as pl
from jax.experimental.pallas import tpu as pltpu
from jax.sharding import PartitionSpec as P

F32, BF16, I32 = jnp.float32, jnp.bfloat16, jnp.int32
SLOT = 16
SIDE = 14
EXTRA = 16
INTERPRET = False
VMEM, SMEM, HBM = pltpu.VMEM, pltpu.SMEM, pltpu.HBM
PIN = object()
DMA = pltpu.SemaphoreType.DMA
LANES = 128
PARTS = 4

NN = (((1,), (0,)), ((), ()))
NT = (((1,), (1,)), ((), ()))
TN = (((0,), (0,)), ((), ()))


def mm(a, b, dims=NN):
    return lax.dot_general(a, b, dims, preferred_element_type=F32)


def iota(shape, dim):
    return lax.broadcasted_iota(I32, shape, dim)


def ones_where(mask):
    return jnp.where(mask, 1.0, 0.0).astype(BF16)


def call(kernel, out_shape, ins=None, outs=None, scratch=(), flops=0, nbytes=0, vmem=32):
    kinds = outs or [VMEM] * len(out_shape)
    forced = {HBM: HBM, PIN: VMEM}

    def run(*args):
        spaces = ins or [VMEM] * len(args)
        args = [pltpu.with_memory_space_constraint(a, forced[m]) if m in forced else a for a, m in zip(args, spaces)]
        return pl.pallas_call(
            kernel,
            out_shape=[forced[m](o.shape, o.dtype) if m in forced else o for o, m in zip(out_shape, kinds)],
            in_specs=[pl.BlockSpec(memory_space=forced.get(m, m)) for m in spaces],
            out_specs=[pl.BlockSpec(memory_space=forced.get(m, m)) for m in kinds],
            scratch_shapes=list(scratch),
            compiler_params=pltpu.CompilerParams(vmem_limit_bytes=vmem * 2**20),
            cost_estimate=pl.CostEstimate(flops=flops, bytes_accessed=nbytes, transcendentals=0),
            interpret=INTERPRET,
        )(*args)

    return run


def sds(shape, dtype):
    return jax.ShapeDtypeStruct(shape, dtype)


def pick_side(arms):
    shape = (arms, arms * SLOT)
    return ones_where(iota(shape, 1) == iota(shape, 0) * SLOT + SIDE)


def column(row):
    return jnp.transpose(jnp.broadcast_to(row, (LANES, row.shape[1])))


def pack_kernel(
    arms, ids_hbm, outcome_hbm, weight_hbm, rep_hbm, slots_hbm, aux_ref,
    ids_ref, outcome_ref, weight_ref, rep_ref, slots_ref, in_sem, out_sem,
):
    pairs = ((ids_hbm, ids_ref), (outcome_hbm, outcome_ref), (weight_hbm, weight_ref), (rep_hbm, rep_ref))
    loads = [pltpu.make_async_copy(a, b, in_sem.at[i]) for i, (a, b) in enumerate(pairs)]
    for load in loads:
        load.start()
    rows, width = rep_ref.shape
    earlier = ones_where(iota((rows, rows), 0) < iota((rows, rows), 1))
    loads[0].wait()
    ids = ids_ref[...]
    hot = iota((arms, rows), 0) == ids
    hot_half = ones_where(hot)
    counts = mm(hot_half, earlier)
    rank = jnp.sum(jnp.where(hot, counts, 0.0), axis=0, keepdims=True).astype(I32)
    slot = ids * SLOT + rank
    row8 = iota((8, rows), 0)
    aux_ref[...] = jnp.where(row8 == 0, slot, jnp.where(row8 == 1, rank, ids))
    lane = iota((width, rows), 0)
    loads[1].wait()
    loads[2].wait()
    outcome = outcome_ref[...].astype(F32).reshape(1, rows)
    weight = weight_ref[...].astype(F32).reshape(1, rows)
    side_t = jnp.where(lane == rank, outcome, 0.0) + jnp.where(lane == rank + SLOT, weight, 0.0)
    side = mm(hot_half, side_t.astype(BF16), NT).astype(BF16)
    loads[3].wait()
    rep = rep_ref[...]
    stores = []
    part = arms * SLOT // PARTS
    for i in range(PARTS):
        place = ones_where(iota((part, rows), 0) + i * part == slot)
        mark = ones_where(iota((part, arms), 0) + i * part == iota((part, arms), 1) * SLOT + SIDE)
        cut = pl.ds(i * part, part)
        slots_ref[cut, :] = (mm(place, rep) + mm(mark, side)).astype(BF16)
        stores.append(pltpu.make_async_copy(slots_ref.at[cut], slots_hbm.at[cut], out_sem.at[i]))
        stores[-1].start()
    for store in stores:
        store.wait()


def side_of(slots, arms):
    return mm(pick_side(arms), slots)


def compact_kernel(arms, packed, slots_ref, send_hbm, pos_ref, side_ref, rows_ref, sem):
    total, width = arms * SLOT, slots_ref.shape[2]
    side = slots_ref[:, SIDE, :].astype(F32)
    slots = slots_ref[...].reshape(total, width)
    side_ref[...] = side.astype(BF16)
    lane8 = iota((8, width), 1)
    weight_lanes = ones_where((lane8 >= SLOT) & (lane8 < 2 * SLOT))
    counts = mm(weight_lanes, ones_where(side > 0.0), NT).astype(BF16)
    source, owner = iota((arms, total), 0), iota((arms, total), 1) // SLOT
    start = mm(counts, ones_where(source < owner))
    count = mm(counts, ones_where(source == owner))
    depth = iota((8, total), 1) % SLOT
    pos = jnp.where(depth < count.astype(I32), start.astype(I32) + depth, 2 * packed)
    pos_ref[...] = pos
    half = packed // 2
    blocks = send_hbm.shape[0]
    stores = []
    for h in range(2):
        gather = ones_where(iota((half, total), 0) + h * half == pos[0:1])
        rows_ref[h] = mm(gather, slots).astype(BF16)
        for d in range(h, blocks, 2):
            stores.append(pltpu.make_async_copy(rows_ref.at[h], send_hbm.at[d], sem.at[d]))
            stores[-1].start()
    for store in stores:
        store.wait()


def prepare_kernel(arms, packed, given_ref, pos_ref, far_hbm, side_ref, far_ref, sem):
    copy = pltpu.make_async_copy(far_hbm, far_ref, sem)
    copy.start()
    total, width = arms * SLOT, given_ref.shape[1]
    side = given_ref[...]
    gather = ones_where(iota((packed, total), 0) == pos_ref[0:1])
    same = iota((arms, total), 0) == iota((arms, total), 1) // SLOT
    lane, place = iota((width, total), 0), iota((width, total), 1) % SLOT
    target = mm(side, ones_where(lane == place))
    weight = mm(side, ones_where(lane == place + SLOT))
    target = jnp.sum(jnp.where(same, target, 0.0), axis=0, keepdims=True)
    weight = jnp.sum(jnp.where(same, weight, 0.0), axis=0, keepdims=True)
    both = jnp.where(iota((8, total), 0) == 0, target, weight)
    side_ref[...] = mm(both.astype(BF16), gather, NT)
    copy.wait()


def unit(pre, head):
    sig = jax.nn.sigmoid(pre)
    return pre * sig, head * sig * (1.0 + pre * (1.0 - sig))


def forward_kernel(
    x_ref, near_ref, far_ref, bh_ref, far_bh_ref, msg_hbm,
    msg_ref, out_sem,
):
    blocks, rows, width = x_ref.shape
    head, far_head = bh_ref[1:2], far_bh_ref[1:2]
    pre = sum(mm(x_ref[j], near_ref[j]) for j in range(blocks)) + bh_ref[0:1]
    act, g = unit(pre, head)
    g = g.astype(BF16)
    pre = sum(mm(x_ref[j], far_ref[j]) for j in range(blocks)) + far_bh_ref[0:1]
    far_act, far_g = unit(pre, far_head)
    far_g = far_g.astype(BF16)
    stores = []
    share = act * head + far_act * far_head
    cut = min(LANES, width)
    share = sum(share[:, i : i + cut] for i in range(0, width, cut))
    share = jnp.sum(jnp.transpose(share), axis=0, keepdims=True)
    high = share.astype(BF16).astype(F32)
    row = iota((EXTRA, rows), 0)
    extra = jnp.where(row == 0, high, jnp.where(row == 1, share - high, 0.0)).astype(BF16)
    for j in range(blocks):
        part = mm(g, near_ref[j], NT) + mm(far_g, far_ref[j], NT)
        msg_ref[j, pl.ds(0, rows), :] = part.astype(BF16)
        msg_ref[j, pl.ds(rows, EXTRA), pl.ds(0, rows)] = extra
        stores.append(pltpu.make_async_copy(msg_ref.at[j], msg_hbm.at[j], out_sem.at[j]))
        stores[-1].start()
    for store in stores:
        store.wait()


def back_kernel(arms, bias_ref, got_ref, side_ref, pos_ref, slots_hbm, resid_ref, slots_ref, sem):
    blocks, rows, width = got_ref.shape
    rows = rows - EXTRA
    total = arms * SLOT
    preds, grads = [], []
    for half in range(2):
        extra = sum(got_ref[j, pl.ds(rows, EXTRA), pl.ds(0, rows)].astype(F32) for j in range(half, blocks, 2))
        preds.append(extra[0:1] + extra[1:2])
        grads.append(sum(got_ref[j, pl.ds(0, rows), :].astype(F32) for j in range(half, blocks, 2)))
    pred = jnp.concatenate(preds, axis=1) + bias_ref[0]
    resid = side_ref[1:2] * (pred - side_ref[0:1])
    resid_ref[...] = jnp.broadcast_to(resid, resid_ref.shape)
    grad = (jnp.concatenate(grads, axis=0) * column(resid)[:, 0:1]).astype(BF16)
    pred = jnp.broadcast_to(pred, (8, 2 * rows)).astype(BF16)
    stores = []
    part = total // PARTS
    for i in range(PARTS):
        cut = pl.ds(i * part, part)
        gather = ones_where(iota((2 * rows, part), 0) == pos_ref[0:1, i * part : (i + 1) * part])
        pred_slot = mm(pred, gather)[0:1]
        row, slot = iota((part, part), 0), iota((part, part), 1)
        spread = jnp.where((row % SLOT == SIDE) & (row // SLOT == slot // SLOT), pred_slot, 0.0).astype(BF16)
        lane = ones_where(iota((width, part), 0) == iota((width, part), 1) % SLOT)
        slots_ref[cut, :] = (mm(gather, grad, TN) + mm(spread, lane, NT)).astype(BF16)
        stores.append(pltpu.make_async_copy(slots_ref.at[cut], slots_hbm.at[cut], sem.at[i]))
        stores[-1].start()
    for store in stores:
        store.wait()


def unpack_kernel(arms, slots_ref, aux_ref, grad_ref, pred_ref):
    total, width = slots_ref.shape
    rows = aux_ref.shape[1]
    slots = slots_ref[...]
    place = ones_where(iota((total, rows), 0) == aux_ref[0:1])
    grad_ref[...] = mm(place, slots, TN).astype(BF16)
    pred_side = side_of(slots, arms).astype(BF16)
    by_arm = mm(pred_side, ones_where(iota((width, rows), 0) == aux_ref[1:2]))
    hot = iota((arms, rows), 0) == aux_ref[2:3]
    pred = jnp.sum(jnp.where(hot, by_arm, 0.0), axis=0, keepdims=True)
    pred_ref[...] = pred.reshape(rows).astype(BF16)


def grads_kernel(core_ref, x_ref, far_x_ref, near_ref, bh_ref, resid_ref, matrix_ref, bias_ref, head_ref, scalar_ref):
    first = core_ref[0] == 0
    blocks, half, _ = x_ref.shape
    low, high = resid_ref[0:1, 0:half], resid_ref[0:1, half : 2 * half]
    scalar_ref[0] = jnp.sum(resid_ref[0:1])
    mine = column(jnp.where(first, low, high))[:, 0:1]
    other = column(jnp.where(first, high, low))[:, 0:1]
    pre_half, bias, head = [], 0.0, 0.0
    for rows_ref, resid in ((x_ref, mine), (far_x_ref, other)):
        pre = sum(mm(rows_ref[j], near_ref[j]) for j in range(blocks)) + bh_ref[0:1]
        act, g = unit(pre, bh_ref[1:2])
        pre_grad = g * resid
        bias += jnp.sum(pre_grad, axis=0, keepdims=True)
        head += jnp.sum(act * resid, axis=0, keepdims=True)
        pre_half.append(pre_grad.astype(BF16))
    bias_ref[...] = bias
    head_ref[...] = head
    for j in range(blocks):
        matrix_ref[j] = mm(x_ref[j], pre_half[0], TN) + mm(far_x_ref[j], pre_half[1], TN)


def body(rep, arm_ids, outcome, weight, w_hidden, b_hidden, w_head, b_head):
    arms = lax.axis_size("dp")
    tower = lax.axis_size("tower")
    rows, width = rep.shape
    packed = 2 * rows
    total = arms * SLOT
    hidden = w_hidden.shape[2]
    core = (lax.axis_index("tower") % 2).astype(I32).reshape(1)

    def swap(value):
        return lax.ppermute(value, "tower", [(i, i ^ 1) for i in range(tower)])

    def exchange(slots):
        cut = slots.reshape(arms, SLOT, width)
        return lax.all_to_all(cut, "dp", split_axis=0, concat_axis=0, tiled=True).reshape(total, width)

    def spread(blocks):
        return lax.all_to_all(blocks, "tower", split_axis=0, concat_axis=0, tiled=True)

    slots, aux = call(
        functools.partial(pack_kernel, arms),
        (sds((total, width), BF16), sds((8, rows), I32)),
        ins=[HBM] * 4,
        outs=[HBM, VMEM],
        scratch=[
            VMEM((1, rows), I32), VMEM((rows,), BF16), VMEM((rows,), BF16), VMEM((rows, width), BF16),
            VMEM((total, width), BF16), DMA((4,)), DMA((PARTS,)),
        ],
        flops=2 * total * rows * width,
    )(arm_ids.reshape(1, rows), outcome, weight, rep)
    arrived = exchange(slots)
    send, pos, given = call(
        functools.partial(compact_kernel, arms, packed),
        (sds((tower, rows, width), BF16), sds((8, total), I32), sds((arms, width), BF16)),
        outs=[HBM, VMEM, VMEM],
        scratch=[VMEM((2, rows, width), BF16), DMA((tower,))],
        flops=2 * total * packed * width,
    )(arrived.reshape(arms, SLOT, width))
    matrix = w_hidden.reshape(tower, width, hidden)
    both = jnp.concatenate([b_hidden, w_head], axis=0)
    inputs = spread(send)
    far_matrix, far_both = swap(matrix), swap(both)
    side, far_matrix = call(
        functools.partial(prepare_kernel, arms, packed),
        (sds((8, packed), F32), sds((tower, width, hidden), BF16)),
        ins=[VMEM, VMEM, HBM],
        outs=[VMEM, PIN],
        scratch=[DMA],
        flops=4 * total * packed * arms,
    )(given, pos, far_matrix)
    (msg,) = call(
        forward_kernel,
        (sds((tower, rows + EXTRA, width), BF16),),
        ins=[VMEM, VMEM, PIN, VMEM, VMEM],
        outs=[HBM],
        scratch=[
            VMEM((tower, rows + EXTRA, width), BF16), DMA((tower,)),
        ],
        flops=8 * rows * tower * width * hidden,
    )(inputs, matrix, far_matrix, both, far_both)
    got = spread(msg)
    msg, inputs2 = lax.optimization_barrier((msg, inputs))
    far_inputs = swap(inputs2)
    back_slots, resid = call(
        functools.partial(back_kernel, arms),
        (sds((total, width), BF16), sds((8, packed), F32)),
        ins=[SMEM, VMEM, VMEM, VMEM],
        outs=[HBM, VMEM],
        scratch=[VMEM((total, width), BF16), DMA((PARTS,))],
        flops=2 * total * packed * width,
    )(b_head, got, side, pos)
    returned = exchange(back_slots)
    grad_matrix, grad_bias, grad_vector, grad_scalar = call(
        grads_kernel,
        (
            sds((tower, width, hidden), F32),
            sds((1, hidden), F32),
            sds((1, hidden), F32),
            sds((1,), F32),
        ),
        ins=[SMEM] + [VMEM] * 5,
        outs=[VMEM, VMEM, VMEM, SMEM],
        flops=4 * packed * tower * width * hidden,
        nbytes=5 * 2**20,
    )(core, inputs, far_inputs, matrix, both, resid)
    grad_rep, predicted = call(
        functools.partial(unpack_kernel, arms),
        (sds((rows, width), BF16), sds((rows,), BF16)),
        flops=2 * total * rows * width,
    )(returned, aux)
    return (
        grad_matrix.reshape(1, tower * width, hidden),
        grad_bias,
        grad_vector,
        grad_scalar,
        grad_rep,
        predicted,
    )


def solution(mesh):
    return jax.shard_map(
        body,
        mesh=mesh,
        in_specs=(
            P("dp", "tower"),
            P("dp"),
            P("dp"),
            P("dp"),
            P("dp", None, "tower"),
            P("dp", "tower"),
            P("dp", "tower"),
            P("dp"),
        ),
        out_specs=(
            P("dp", None, "tower"),
            P("dp", "tower"),
            P("dp", "tower"),
            P("dp"),
            P("dp", "tower"),
            P("dp"),
        ),
        check_vma=False,
    )
```

```python
import functools

import jax
import jax.numpy as jnp
from jax import lax
from jax.experimental import pallas as pl
from jax.experimental.pallas import tpu as pltpu
from jax.sharding import PartitionSpec as P

F32, BF16, I32 = jnp.float32, jnp.bfloat16, jnp.int32
SLOT = 16
SIDE = 14
EXTRA = 16
INTERPRET = False
VMEM, SMEM, HBM = pltpu.VMEM, pltpu.SMEM, pltpu.HBM
PIN = object()
DMA = pltpu.SemaphoreType.DMA
LANES = 128
PARTS = 4

NN = (((1,), (0,)), ((), ()))
NT = (((1,), (1,)), ((), ()))
TN = (((0,), (0,)), ((), ()))


def mm(a, b, dims=NN):
    return lax.dot_general(a, b, dims, preferred_element_type=F32)


def iota(shape, dim):
    return lax.broadcasted_iota(I32, shape, dim)


def ones_where(mask):
    return jnp.where(mask, 1.0, 0.0).astype(BF16)


def call(kernel, out_shape, ins=None, outs=None, scratch=(), flops=0, nbytes=0, vmem=32):
    kinds = outs or [VMEM] * len(out_shape)
    forced = {HBM: HBM, PIN: VMEM}

    def run(*args):
        spaces = ins or [VMEM] * len(args)
        args = [pltpu.with_memory_space_constraint(a, forced[m]) if m in forced else a for a, m in zip(args, spaces)]
        return pl.pallas_call(
            kernel,
            out_shape=[forced[m](o.shape, o.dtype) if m in forced else o for o, m in zip(out_shape, kinds)],
            in_specs=[pl.BlockSpec(memory_space=forced.get(m, m)) for m in spaces],
            out_specs=[pl.BlockSpec(memory_space=forced.get(m, m)) for m in kinds],
            scratch_shapes=list(scratch),
            compiler_params=pltpu.CompilerParams(vmem_limit_bytes=vmem * 2**20),
            cost_estimate=pl.CostEstimate(flops=flops, bytes_accessed=nbytes, transcendentals=0),
            interpret=INTERPRET,
        )(*args)

    return run


def sds(shape, dtype):
    return jax.ShapeDtypeStruct(shape, dtype)


def pick_side(arms):
    shape = (arms, arms * SLOT)
    return ones_where(iota(shape, 1) == iota(shape, 0) * SLOT + SIDE)


def column(row):
    return jnp.transpose(jnp.broadcast_to(row, (LANES, row.shape[1])))


def pack_kernel(
    arms, ids_hbm, outcome_hbm, weight_hbm, rep_hbm, slots_hbm, aux_ref,
    ids_ref, outcome_ref, weight_ref, rep_ref, slots_ref, in_sem, out_sem,
):
    pairs = ((ids_hbm, ids_ref), (outcome_hbm, outcome_ref), (weight_hbm, weight_ref), (rep_hbm, rep_ref))
    loads = [pltpu.make_async_copy(a, b, in_sem.at[i]) for i, (a, b) in enumerate(pairs)]
    for load in loads:
        load.start()
    rows, width = rep_ref.shape
    earlier = ones_where(iota((rows, rows), 0) < iota((rows, rows), 1))
    loads[0].wait()
    ids = ids_ref[...]
    hot = iota((arms, rows), 0) == ids
    hot_half = ones_where(hot)
    counts = mm(hot_half, earlier)
    rank = jnp.sum(jnp.where(hot, counts, 0.0), axis=0, keepdims=True).astype(I32)
    slot = ids * SLOT + rank
    row8 = iota((8, rows), 0)
    aux_ref[...] = jnp.where(row8 == 0, slot, jnp.where(row8 == 1, rank, ids))
    lane = iota((width, rows), 0)
    loads[1].wait()
    loads[2].wait()
    outcome = outcome_ref[...].astype(F32).reshape(1, rows)
    weight = weight_ref[...].astype(F32).reshape(1, rows)
    side_t = jnp.where(lane == rank, outcome, 0.0) + jnp.where(lane == rank + SLOT, weight, 0.0)
    side = mm(hot_half, side_t.astype(BF16), NT).astype(BF16)
    loads[3].wait()
    rep = rep_ref[...]
    stores = []
    part = arms * SLOT // PARTS
    for i in range(PARTS):
        place = ones_where(iota((part, rows), 0) + i * part == slot)
        mark = ones_where(iota((part, arms), 0) + i * part == iota((part, arms), 1) * SLOT + SIDE)
        cut = pl.ds(i * part, part)
        slots_ref[cut, :] = (mm(place, rep) + mm(mark, side)).astype(BF16)
        stores.append(pltpu.make_async_copy(slots_ref.at[cut], slots_hbm.at[cut], out_sem.at[i]))
        stores[-1].start()
    for store in stores:
        store.wait()


def side_of(slots, arms):
    return mm(pick_side(arms), slots)


def compact_kernel(arms, packed, slots_ref, send_ref, pos_ref, side_ref):
    total, width = arms * SLOT, slots_ref.shape[2]
    side = slots_ref[:, SIDE, :].astype(F32)
    slots = slots_ref[...].reshape(total, width)
    side_ref[...] = side.astype(BF16)
    lane8 = iota((8, width), 1)
    weight_lanes = ones_where((lane8 >= SLOT) & (lane8 < 2 * SLOT))
    counts = mm(weight_lanes, ones_where(side > 0.0), NT).astype(BF16)
    source, owner = iota((arms, total), 0), iota((arms, total), 1) // SLOT
    start = mm(counts, ones_where(source < owner))
    count = mm(counts, ones_where(source == owner))
    depth = iota((8, total), 1) % SLOT
    pos = jnp.where(depth < count.astype(I32), start.astype(I32) + depth, 2 * packed)
    pos_ref[...] = pos
    half = packed // 2
    for h in range(2):
        gather = ones_where(iota((half, total), 0) + h * half == pos[0:1])
        rows = mm(gather, slots).astype(BF16)
        for d in range(h, send_ref.shape[0], 2):
            send_ref[d] = rows


def prepare_kernel(arms, packed, given_ref, pos_ref, side_ref):
    total, width = arms * SLOT, given_ref.shape[1]
    side = given_ref[...]
    gather = ones_where(iota((packed, total), 0) == pos_ref[0:1])
    same = iota((arms, total), 0) == iota((arms, total), 1) // SLOT
    lane, place = iota((width, total), 0), iota((width, total), 1) % SLOT
    target = mm(side, ones_where(lane == place))
    weight = mm(side, ones_where(lane == place + SLOT))
    target = jnp.sum(jnp.where(same, target, 0.0), axis=0, keepdims=True)
    weight = jnp.sum(jnp.where(same, weight, 0.0), axis=0, keepdims=True)
    both = jnp.where(iota((8, total), 0) == 0, target, weight)
    side_ref[...] = mm(both.astype(BF16), gather, NT)


def unit(pre, head):
    sig = jax.nn.sigmoid(pre)
    return pre * sig, head * sig * (1.0 + pre * (1.0 - sig))


def forward_kernel(
    x_ref, near_ref, far_ref, bh_ref, far_bh_ref, msg_hbm,
    msg_ref, out_sem,
):
    blocks, rows, width = x_ref.shape
    head, far_head = bh_ref[1:2], far_bh_ref[1:2]
    pre = sum(mm(x_ref[j], near_ref[j]) for j in range(blocks)) + bh_ref[0:1]
    act, g = unit(pre, head)
    g = g.astype(BF16)
    pre = sum(mm(x_ref[j], far_ref[j]) for j in range(blocks)) + far_bh_ref[0:1]
    far_act, far_g = unit(pre, far_head)
    far_g = far_g.astype(BF16)
    stores = []
    share = act * head + far_act * far_head
    cut = min(LANES, width)
    share = sum(share[:, i : i + cut] for i in range(0, width, cut))
    share = jnp.sum(jnp.transpose(share), axis=0, keepdims=True)
    high = share.astype(BF16).astype(F32)
    row = iota((EXTRA, rows), 0)
    extra = jnp.where(row == 0, high, jnp.where(row == 1, share - high, 0.0)).astype(BF16)
    for j in range(blocks):
        part = mm(g, near_ref[j], NT) + mm(far_g, far_ref[j], NT)
        msg_ref[j, pl.ds(0, rows), :] = part.astype(BF16)
        msg_ref[j, pl.ds(rows, EXTRA), pl.ds(0, rows)] = extra
        stores.append(pltpu.make_async_copy(msg_ref.at[j], msg_hbm.at[j], out_sem.at[j]))
        stores[-1].start()
    for store in stores:
        store.wait()


def back_kernel(arms, bias_ref, got_ref, side_ref, pos_ref, slots_hbm, resid_ref, slots_ref, sem):
    blocks, rows, width = got_ref.shape
    rows = rows - EXTRA
    total = arms * SLOT
    preds, grads = [], []
    for half in range(2):
        extra = sum(got_ref[j, pl.ds(rows, EXTRA), pl.ds(0, rows)].astype(F32) for j in range(half, blocks, 2))
        preds.append(extra[0:1] + extra[1:2])
        grads.append(sum(got_ref[j, pl.ds(0, rows), :].astype(F32) for j in range(half, blocks, 2)))
    pred = jnp.concatenate(preds, axis=1) + bias_ref[0]
    resid = side_ref[1:2] * (pred - side_ref[0:1])
    resid_ref[...] = jnp.broadcast_to(resid, resid_ref.shape)
    grad = (jnp.concatenate(grads, axis=0) * column(resid)[:, 0:1]).astype(BF16)
    pred = jnp.broadcast_to(pred, (8, 2 * rows)).astype(BF16)
    stores = []
    part = total // PARTS
    for i in range(PARTS):
        cut = pl.ds(i * part, part)
        gather = ones_where(iota((2 * rows, part), 0) == pos_ref[0:1, i * part : (i + 1) * part])
        pred_slot = mm(pred, gather)[0:1]
        row, slot = iota((part, part), 0), iota((part, part), 1)
        spread = jnp.where((row % SLOT == SIDE) & (row // SLOT == slot // SLOT), pred_slot, 0.0).astype(BF16)
        lane = ones_where(iota((width, part), 0) == iota((width, part), 1) % SLOT)
        slots_ref[cut, :] = (mm(gather, grad, TN) + mm(spread, lane, NT)).astype(BF16)
        stores.append(pltpu.make_async_copy(slots_ref.at[cut], slots_hbm.at[cut], sem.at[i]))
        stores[-1].start()
    for store in stores:
        store.wait()


def unpack_kernel(arms, slots_ref, aux_ref, grad_ref, pred_ref):
    total, width = slots_ref.shape
    rows = aux_ref.shape[1]
    slots = slots_ref[...]
    place = ones_where(iota((total, rows), 0) == aux_ref[0:1])
    grad_ref[...] = mm(place, slots, TN).astype(BF16)
    pred_side = side_of(slots, arms).astype(BF16)
    by_arm = mm(pred_side, ones_where(iota((width, rows), 0) == aux_ref[1:2]))
    hot = iota((arms, rows), 0) == aux_ref[2:3]
    pred = jnp.sum(jnp.where(hot, by_arm, 0.0), axis=0, keepdims=True)
    pred_ref[...] = pred.reshape(rows).astype(BF16)


def grads_kernel(core_ref, x_ref, far_x_ref, near_ref, bh_ref, resid_ref, matrix_ref, bias_ref, head_ref, scalar_ref):
    first = core_ref[0] == 0
    blocks, half, _ = x_ref.shape
    low, high = resid_ref[0:1, 0:half], resid_ref[0:1, half : 2 * half]
    scalar_ref[0] = jnp.sum(resid_ref[0:1])
    mine = column(jnp.where(first, low, high))[:, 0:1]
    other = column(jnp.where(first, high, low))[:, 0:1]
    pre_half, bias, head = [], 0.0, 0.0
    for rows_ref, resid in ((x_ref, mine), (far_x_ref, other)):
        pre = sum(mm(rows_ref[j], near_ref[j]) for j in range(blocks)) + bh_ref[0:1]
        act, g = unit(pre, bh_ref[1:2])
        pre_grad = g * resid
        bias += jnp.sum(pre_grad, axis=0, keepdims=True)
        head += jnp.sum(act * resid, axis=0, keepdims=True)
        pre_half.append(pre_grad.astype(BF16))
    bias_ref[...] = bias
    head_ref[...] = head
    for j in range(blocks):
        matrix_ref[j] = mm(x_ref[j], pre_half[0], TN) + mm(far_x_ref[j], pre_half[1], TN)


def body(rep, arm_ids, outcome, weight, w_hidden, b_hidden, w_head, b_head):
    arms = lax.axis_size("dp")
    tower = lax.axis_size("tower")
    rows, width = rep.shape
    packed = 2 * rows
    total = arms * SLOT
    hidden = w_hidden.shape[2]
    core = (lax.axis_index("tower") % 2).astype(I32).reshape(1)

    def swap(value):
        return lax.ppermute(value, "tower", [(i, i ^ 1) for i in range(tower)])

    def exchange(slots):
        cut = slots.reshape(arms, SLOT, width)
        return lax.all_to_all(cut, "dp", split_axis=0, concat_axis=0, tiled=True).reshape(total, width)

    def spread(blocks):
        return lax.all_to_all(blocks, "tower", split_axis=0, concat_axis=0, tiled=True)

    slots, aux = call(
        functools.partial(pack_kernel, arms),
        (sds((total, width), BF16), sds((8, rows), I32)),
        ins=[HBM] * 4,
        outs=[HBM, VMEM],
        scratch=[
            VMEM((1, rows), I32), VMEM((rows,), BF16), VMEM((rows,), BF16), VMEM((rows, width), BF16),
            VMEM((total, width), BF16), DMA((4,)), DMA((PARTS,)),
        ],
        flops=2 * total * rows * width,
    )(arm_ids.reshape(1, rows), outcome, weight, rep)
    matrix = w_hidden.reshape(tower, width, hidden)
    both = jnp.concatenate([b_hidden, w_head], axis=0)
    far_matrix, far_both = swap(matrix), swap(both)
    arrived = exchange(slots)
    arrived, far_both = lax.optimization_barrier((arrived, far_both))
    send, pos, given = call(
        functools.partial(compact_kernel, arms, packed),
        (sds((tower, rows, width), BF16), sds((8, total), I32), sds((arms, width), BF16)),
        flops=2 * total * packed * width,
    )(arrived.reshape(arms, SLOT, width))
    send, far_matrix = lax.optimization_barrier((send, far_matrix))
    inputs = spread(send)
    (msg,) = call(
        forward_kernel,
        (sds((tower, rows + EXTRA, width), BF16),),
        ins=[VMEM] * 5,
        outs=[HBM],
        scratch=[
            VMEM((tower, rows + EXTRA, width), BF16), DMA((tower,)),
        ],
        flops=8 * rows * tower * width * hidden,
    )(inputs, matrix, far_matrix, both, far_both)
    got = spread(msg)
    msg, later, pos, given = lax.optimization_barrier((msg, inputs, pos, given))
    far_inputs = swap(later)
    (side,) = call(
        functools.partial(prepare_kernel, arms, packed),
        (sds((8, packed), F32),),
        flops=4 * total * packed * arms,
    )(given, pos)
    back_slots, resid = call(
        functools.partial(back_kernel, arms),
        (sds((total, width), BF16), sds((8, packed), F32)),
        ins=[SMEM, VMEM, VMEM, VMEM],
        outs=[HBM, VMEM],
        scratch=[VMEM((total, width), BF16), DMA((PARTS,))],
        flops=2 * total * packed * width,
    )(b_head, got, side, pos)
    returned = exchange(back_slots)
    grad_matrix, grad_bias, grad_vector, grad_scalar = call(
        grads_kernel,
        (
            sds((tower, width, hidden), F32),
            sds((1, hidden), F32),
            sds((1, hidden), F32),
            sds((1,), F32),
        ),
        ins=[SMEM] + [VMEM] * 5,
        outs=[VMEM, VMEM, VMEM, SMEM],
        flops=4 * packed * tower * width * hidden,
        nbytes=5 * 2**20,
    )(core, inputs, far_inputs, matrix, both, resid)
    grad_rep, predicted = call(
        functools.partial(unpack_kernel, arms),
        (sds((rows, width), BF16), sds((rows,), BF16)),
        flops=2 * total * rows * width,
    )(returned, aux)
    return (
        grad_matrix.reshape(1, tower * width, hidden),
        grad_bias,
        grad_vector,
        grad_scalar,
        grad_rep,
        predicted,
    )


def solution(mesh):
    return jax.shard_map(
        body,
        mesh=mesh,
        in_specs=(
            P("dp", "tower"),
            P("dp"),
            P("dp"),
            P("dp"),
            P("dp", None, "tower"),
            P("dp", "tower"),
            P("dp", "tower"),
            P("dp"),
        ),
        out_specs=(
            P("dp", None, "tower"),
            P("dp", "tower"),
            P("dp", "tower"),
            P("dp"),
            P("dp", "tower"),
            P("dp"),
        ),
        check_vma=False,
    )
```

```python
import functools

import jax
import jax.numpy as jnp
from jax import lax
from jax.experimental import pallas as pl
from jax.experimental.pallas import tpu as pltpu
from jax.sharding import PartitionSpec as P

F32, BF16, I32 = jnp.float32, jnp.bfloat16, jnp.int32
SLOT = 16
SIDE = 14
INTERPRET = False
VMEM, SMEM, HBM = pltpu.VMEM, pltpu.SMEM, pltpu.HBM
PIN = object()
DMA = pltpu.SemaphoreType.DMA
LANES = 128
PARTS = 4

NN = (((1,), (0,)), ((), ()))
NT = (((1,), (1,)), ((), ()))
TN = (((0,), (0,)), ((), ()))


def mm(a, b, dims=NN):
    return lax.dot_general(a, b, dims, preferred_element_type=F32)


def iota(shape, dim):
    return lax.broadcasted_iota(I32, shape, dim)


def ones_where(mask):
    return jnp.where(mask, 1.0, 0.0).astype(BF16)


def call(kernel, out_shape, ins=None, outs=None, scratch=(), flops=0, nbytes=0, vmem=32):
    kinds = outs or [VMEM] * len(out_shape)
    forced = {HBM: HBM, PIN: VMEM}

    def run(*args):
        spaces = ins or [VMEM] * len(args)
        args = [pltpu.with_memory_space_constraint(a, forced[m]) if m in forced else a for a, m in zip(args, spaces)]
        return pl.pallas_call(
            kernel,
            out_shape=[forced[m](o.shape, o.dtype) if m in forced else o for o, m in zip(out_shape, kinds)],
            in_specs=[pl.BlockSpec(memory_space=forced.get(m, m)) for m in spaces],
            out_specs=[pl.BlockSpec(memory_space=forced.get(m, m)) for m in kinds],
            scratch_shapes=list(scratch),
            compiler_params=pltpu.CompilerParams(vmem_limit_bytes=vmem * 2**20),
            cost_estimate=pl.CostEstimate(flops=flops, bytes_accessed=nbytes, transcendentals=0),
            interpret=INTERPRET,
        )(*args)

    return run


def sds(shape, dtype):
    return jax.ShapeDtypeStruct(shape, dtype)


def pick_side(arms):
    shape = (arms, arms * SLOT)
    return ones_where(iota(shape, 1) == iota(shape, 0) * SLOT + SIDE)


def column(row):
    return jnp.transpose(jnp.broadcast_to(row, (LANES, row.shape[1])))


def pack_kernel(
    arms, ids_hbm, outcome_hbm, weight_hbm, rep_hbm, slots_hbm, aux_ref,
    ids_ref, outcome_ref, weight_ref, rep_ref, slots_ref, in_sem, out_sem,
):
    pairs = ((ids_hbm, ids_ref), (outcome_hbm, outcome_ref), (weight_hbm, weight_ref), (rep_hbm, rep_ref))
    loads = [pltpu.make_async_copy(a, b, in_sem.at[i]) for i, (a, b) in enumerate(pairs)]
    for load in loads:
        load.start()
    rows, width = rep_ref.shape
    earlier = ones_where(iota((rows, rows), 0) < iota((rows, rows), 1))
    loads[0].wait()
    ids = ids_ref[...]
    hot = iota((arms, rows), 0) == ids
    hot_half = ones_where(hot)
    counts = mm(hot_half, earlier)
    rank = jnp.sum(jnp.where(hot, counts, 0.0), axis=0, keepdims=True).astype(I32)
    slot = ids * SLOT + rank
    row8 = iota((8, rows), 0)
    aux_ref[...] = jnp.where(row8 == 0, slot, jnp.where(row8 == 1, rank, ids))
    lane = iota((width, rows), 0)
    loads[1].wait()
    loads[2].wait()
    outcome = outcome_ref[...].astype(F32).reshape(1, rows)
    weight = weight_ref[...].astype(F32).reshape(1, rows)
    side_t = jnp.where(lane == rank, outcome, 0.0) + jnp.where(lane == rank + SLOT, weight, 0.0)
    side = mm(hot_half, side_t.astype(BF16), NT).astype(BF16)
    loads[3].wait()
    rep = rep_ref[...]
    stores = []
    part = arms * SLOT // PARTS
    for i in range(PARTS):
        place = ones_where(iota((part, rows), 0) + i * part == slot)
        cut = pl.ds(i * part, part)
        slots_ref[cut, :] = mm(place, rep).astype(BF16)
        few = part // SLOT
        slots_ref.reshape(arms, SLOT, width)[i * few : (i + 1) * few, SIDE, :] = side[i * few : (i + 1) * few]
        stores.append(pltpu.make_async_copy(slots_ref.at[cut], slots_hbm.at[cut], out_sem.at[i]))
        stores[-1].start()
    for store in stores:
        store.wait()


def side_of(slots, arms):
    return mm(pick_side(arms), slots)


def compact_kernel(arms, packed, slots_ref, send_ref, pos_ref, side_ref):
    total, width = arms * SLOT, slots_ref.shape[2]
    side = slots_ref[:, SIDE, :].astype(F32)
    slots = slots_ref[...].reshape(total, width)
    side_ref[...] = side.astype(BF16)
    lane8 = iota((8, width), 1)
    weight_lanes = ones_where((lane8 >= SLOT) & (lane8 < 2 * SLOT))
    counts = mm(weight_lanes, ones_where(side > 0.0), NT).astype(BF16)
    source, owner = iota((arms, total), 0), iota((arms, total), 1) // SLOT
    start = mm(counts, ones_where(source < owner))
    count = mm(counts, ones_where(source == owner))
    depth = iota((8, total), 1) % SLOT
    pos = jnp.where(depth < count.astype(I32), start.astype(I32) + depth, 2 * packed)
    pos_ref[...] = pos
    half = packed // 2
    for h in range(2):
        gather = ones_where(iota((half, total), 0) + h * half == pos[0:1])
        rows = mm(gather, slots).astype(BF16)
        for d in range(h, send_ref.shape[0], 2):
            send_ref[d] = rows


def plan_kernel(arms, core_ref, bias_ref, mine_ref, other_ref, given_ref, pos_ref, resid_ref, pred_ref):
    first = core_ref[0] == 0
    total, width = arms * SLOT, given_ref.shape[1]
    mine, other = mine_ref[0:1], other_ref[0:1]
    pred = jnp.concatenate([jnp.where(first, mine, other), jnp.where(first, other, mine)], axis=1) + bias_ref[0]
    packed = pred.shape[1]
    side = given_ref[...]
    gather = ones_where(iota((packed, total), 0) == pos_ref[0:1])
    same = iota((arms, total), 0) == iota((arms, total), 1) // SLOT
    lane, place = iota((width, total), 0), iota((width, total), 1) % SLOT
    target = mm(side, ones_where(lane == place))
    weight = mm(side, ones_where(lane == place + SLOT))
    target = jnp.sum(jnp.where(same, target, 0.0), axis=0, keepdims=True)
    weight = jnp.sum(jnp.where(same, weight, 0.0), axis=0, keepdims=True)
    both = jnp.where(iota((8, total), 0) == 0, target, weight)
    both = mm(both.astype(BF16), gather, NT)
    resid_ref[...] = jnp.broadcast_to(both[1:2] * (pred - both[0:1]), resid_ref.shape)
    pred_slot = mm(jnp.broadcast_to(pred, (8, packed)).astype(BF16), gather)
    pred_ref[...] = mm(jnp.where(same, pred_slot[0:1], 0.0).astype(BF16), ones_where(lane == place), NT).astype(BF16)


def unit(pre, head):
    sig = jax.nn.sigmoid(pre)
    return pre * sig, head * sig * (1.0 + pre * (1.0 - sig))


def forward_kernel(
    x_ref, near_ref, far_lo_ref, far_hi_ref, bh_ref, far_bh_ref, msg_hbm, share_ref,
    msg_ref, out_sem,
):
    blocks, rows, width = x_ref.shape
    half = blocks // 2
    far = [far_lo_ref.at[j] for j in range(half)] + [far_hi_ref.at[j] for j in range(half)]
    head, far_head = bh_ref[1:2], far_bh_ref[1:2]
    pre = sum(mm(x_ref[j], near_ref[j]) for j in range(blocks)) + bh_ref[0:1]
    act, g = unit(pre, head)
    g = g.astype(BF16)
    pre = sum(mm(x_ref[j], far[j][...]) for j in range(blocks)) + far_bh_ref[0:1]
    far_act, far_g = unit(pre, far_head)
    far_g = far_g.astype(BF16)
    stores = []
    share = act * head + far_act * far_head
    cut = min(LANES, width)
    share = sum(share[:, i : i + cut] for i in range(0, width, cut))
    share_ref[...] = jnp.broadcast_to(jnp.sum(jnp.transpose(share), axis=0, keepdims=True), share_ref.shape)
    for j in range(blocks):
        part = mm(g, near_ref[j], NT) + mm(far_g, far[j][...], NT)
        msg_ref[j] = part.astype(BF16)
        stores.append(pltpu.make_async_copy(msg_ref.at[j], msg_hbm.at[j], out_sem.at[j]))
        stores[-1].start()
    for store in stores:
        store.wait()


def back_kernel(arms, got_ref, resid_ref, pred_ref, pos_ref, slots_hbm, slots_ref, sem):
    blocks, rows, width = got_ref.shape
    total = arms * SLOT
    grads = [sum(got_ref[j].astype(F32) for j in range(half, blocks, 2)) for half in range(2)]
    grad = (jnp.concatenate(grads, axis=0) * column(resid_ref[0:1])[:, 0:1]).astype(BF16)
    stores = []
    part = total // PARTS
    for i in range(PARTS):
        cut = pl.ds(i * part, part)
        gather = ones_where(iota((2 * rows, part), 0) == pos_ref[0:1, i * part : (i + 1) * part])
        slots_ref[cut, :] = mm(gather, grad, TN).astype(BF16)
        few = part // SLOT
        slots_ref.reshape(arms, SLOT, width)[i * few : (i + 1) * few, SIDE, :] = pred_ref[i * few : (i + 1) * few]
        stores.append(pltpu.make_async_copy(slots_ref.at[cut], slots_hbm.at[cut], sem.at[i]))
        stores[-1].start()
    for store in stores:
        store.wait()


def unpack_kernel(arms, slots_ref, aux_ref, grad_ref, pred_ref):
    total, width = slots_ref.shape
    rows = aux_ref.shape[1]
    slots = slots_ref[...]
    place = ones_where(iota((total, rows), 0) == aux_ref[0:1])
    grad_ref[...] = mm(place, slots, TN).astype(BF16)
    pred_side = slots_ref.reshape(arms, SLOT, width)[:, SIDE, :]
    by_arm = mm(pred_side, ones_where(iota((width, rows), 0) == aux_ref[1:2]))
    hot = iota((arms, rows), 0) == aux_ref[2:3]
    pred = jnp.sum(jnp.where(hot, by_arm, 0.0), axis=0, keepdims=True)
    pred_ref[...] = pred.reshape(rows).astype(BF16)


def grads_kernel(core_ref, x_ref, far_x_ref, near_ref, bh_ref, resid_ref, matrix_ref, bias_ref, head_ref, scalar_ref):
    first = core_ref[0] == 0
    blocks, half, _ = x_ref.shape
    low, high = resid_ref[0:1, 0:half], resid_ref[0:1, half : 2 * half]
    scalar_ref[0] = jnp.sum(resid_ref[0:1])
    mine = column(jnp.where(first, low, high))[:, 0:1]
    other = column(jnp.where(first, high, low))[:, 0:1]
    pre_half, bias, head = [], 0.0, 0.0
    for rows_ref, resid in ((x_ref, mine), (far_x_ref, other)):
        pre = sum(mm(rows_ref[j], near_ref[j]) for j in range(blocks)) + bh_ref[0:1]
        act, g = unit(pre, bh_ref[1:2])
        pre_grad = g * resid
        bias += jnp.sum(pre_grad, axis=0, keepdims=True)
        head += jnp.sum(act * resid, axis=0, keepdims=True)
        pre_half.append(pre_grad.astype(BF16))
    bias_ref[...] = bias
    head_ref[...] = head
    for j in range(blocks):
        matrix_ref[j] = mm(x_ref[j], pre_half[0], TN) + mm(far_x_ref[j], pre_half[1], TN)


def body(rep, arm_ids, outcome, weight, w_hidden, b_hidden, w_head, b_head):
    arms = lax.axis_size("dp")
    tower = lax.axis_size("tower")
    rows, width = rep.shape
    packed = 2 * rows
    total = arms * SLOT
    hidden = w_hidden.shape[2]
    core = (lax.axis_index("tower") % 2).astype(I32).reshape(1)

    def hop(value, by):
        return lax.ppermute(value, "tower", [(i, (i + 2 * by) % tower) for i in range(tower)])

    def swap(value):
        return lax.ppermute(value, "tower", [(i, i ^ 1) for i in range(tower)])

    def exchange(slots):
        cut = slots.reshape(arms, SLOT, width)
        return lax.all_to_all(cut, "dp", split_axis=0, concat_axis=0, tiled=True).reshape(total, width)

    def spread(blocks):
        return lax.all_to_all(blocks, "tower", split_axis=0, concat_axis=0, tiled=True)

    slots, aux = call(
        functools.partial(pack_kernel, arms),
        (sds((total, width), BF16), sds((8, rows), I32)),
        ins=[HBM] * 4,
        outs=[HBM, VMEM],
        scratch=[
            VMEM((1, rows), I32), VMEM((rows,), BF16), VMEM((rows,), BF16), VMEM((rows, width), BF16),
            VMEM((total, width), BF16), DMA((4,)), DMA((PARTS,)),
        ],
        flops=2 * total * rows * width,
    )(arm_ids.reshape(1, rows), outcome, weight, rep)
    matrix = w_hidden.reshape(tower, width, hidden)
    both = jnp.concatenate([b_hidden, w_head], axis=0)
    far_lo, far_hi, far_both = swap(matrix[: tower // 2]), swap(matrix[tower // 2 :]), swap(both)
    arrived = exchange(slots)
    arrived, far_lo, far_hi, far_both = lax.optimization_barrier((arrived, far_lo, far_hi, far_both))
    send, pos, given = call(
        functools.partial(compact_kernel, arms, packed),
        (sds((tower, rows, width), BF16), sds((8, total), I32), sds((arms, width), BF16)),
        flops=2 * total * packed * width,
    )(arrived.reshape(arms, SLOT, width))
    inputs = spread(send)
    msg, share = call(
        forward_kernel,
        (sds((tower, rows, width), BF16), sds((8, rows), F32)),
        ins=[VMEM] * 6,
        outs=[HBM, VMEM],
        scratch=[
            VMEM((tower, rows, width), BF16), DMA((tower,)),
        ],
        flops=8 * rows * tower * width * hidden,
    )(inputs, matrix, far_lo, far_hi, both, far_both)
    got = spread(msg)
    msg, later, pos, given, share = lax.optimization_barrier((msg, inputs, pos, given, share))
    mine = (share + hop(share, 2)) + (hop(share, 1) + hop(share, -1))
    resid, pred_side = call(
        functools.partial(plan_kernel, arms),
        (sds((8, packed), F32), sds((arms, width), BF16)),
        ins=[SMEM, SMEM] + [VMEM] * 4,
        flops=4 * total * packed * arms,
    )(core, b_head, mine, swap(mine), given, pos)
    far_inputs = swap(later)
    (back_slots,) = call(
        functools.partial(back_kernel, arms),
        (sds((total, width), BF16),),
        outs=[HBM],
        scratch=[VMEM((total, width), BF16), DMA((PARTS,))],
        flops=2 * total * packed * width,
    )(got, resid, pred_side, pos)
    returned = exchange(back_slots)
    grad_matrix, grad_bias, grad_vector, grad_scalar = call(
        grads_kernel,
        (
            sds((tower, width, hidden), F32),
            sds((1, hidden), F32),
            sds((1, hidden), F32),
            sds((1,), F32),
        ),
        ins=[SMEM] + [VMEM] * 5,
        outs=[VMEM, VMEM, VMEM, SMEM],
        flops=4 * packed * tower * width * hidden,
        nbytes=5 * 2**20,
    )(core, inputs, far_inputs, matrix, both, resid)
    grad_rep, predicted = call(
        functools.partial(unpack_kernel, arms),
        (sds((rows, width), BF16), sds((rows,), BF16)),
        flops=2 * total * rows * width,
    )(returned, aux)
    return (
        grad_matrix.reshape(1, tower * width, hidden),
        grad_bias,
        grad_vector,
        grad_scalar,
        grad_rep,
        predicted,
    )


def solution(mesh):
    return jax.shard_map(
        body,
        mesh=mesh,
        in_specs=(
            P("dp", "tower"),
            P("dp"),
            P("dp"),
            P("dp"),
            P("dp", None, "tower"),
            P("dp", "tower"),
            P("dp", "tower"),
            P("dp"),
        ),
        out_specs=(
            P("dp", None, "tower"),
            P("dp", "tower"),
            P("dp", "tower"),
            P("dp"),
            P("dp", "tower"),
            P("dp"),
        ),
        check_vma=False,
    )
```

```python
import functools

import jax
import jax.numpy as jnp
from jax import lax
from jax.experimental import pallas as pl
from jax.experimental.pallas import tpu as pltpu
from jax.sharding import PartitionSpec as P

F32, BF16, I32 = jnp.float32, jnp.bfloat16, jnp.int32
SLOT = 16
SIDE = 14
EXTRA = 16
INTERPRET = False
VMEM, SMEM, HBM = pltpu.VMEM, pltpu.SMEM, pltpu.HBM
PIN = object()
DMA = pltpu.SemaphoreType.DMA
LANES = 128
PARTS = 4

NN = (((1,), (0,)), ((), ()))
NT = (((1,), (1,)), ((), ()))
TN = (((0,), (0,)), ((), ()))


def mm(a, b, dims=NN):
    return lax.dot_general(a, b, dims, preferred_element_type=F32)


def iota(shape, dim):
    return lax.broadcasted_iota(I32, shape, dim)


def ones_where(mask):
    return jnp.where(mask, 1.0, 0.0).astype(BF16)


def call(kernel, out_shape, ins=None, outs=None, scratch=(), flops=0, nbytes=0, vmem=32):
    kinds = outs or [VMEM] * len(out_shape)
    forced = {HBM: HBM, PIN: VMEM}

    def run(*args):
        spaces = ins or [VMEM] * len(args)
        args = [pltpu.with_memory_space_constraint(a, forced[m]) if m in forced else a for a, m in zip(args, spaces)]
        return pl.pallas_call(
            kernel,
            out_shape=[forced[m](o.shape, o.dtype) if m in forced else o for o, m in zip(out_shape, kinds)],
            in_specs=[pl.BlockSpec(memory_space=forced.get(m, m)) for m in spaces],
            out_specs=[pl.BlockSpec(memory_space=forced.get(m, m)) for m in kinds],
            scratch_shapes=list(scratch),
            compiler_params=pltpu.CompilerParams(vmem_limit_bytes=vmem * 2**20),
            cost_estimate=pl.CostEstimate(flops=flops, bytes_accessed=nbytes, transcendentals=0),
            interpret=INTERPRET,
        )(*args)

    return run


def sds(shape, dtype):
    return jax.ShapeDtypeStruct(shape, dtype)


def pick_side(arms):
    shape = (arms, arms * SLOT)
    return ones_where(iota(shape, 1) == iota(shape, 0) * SLOT + SIDE)


def column(row):
    return jnp.transpose(jnp.broadcast_to(row, (LANES, row.shape[1])))


def pack_kernel(
    arms, ids_hbm, outcome_hbm, weight_hbm, rep_hbm, slots_hbm, aux_ref,
    ids_ref, outcome_ref, weight_ref, rep_ref, slots_ref, in_sem, out_sem,
):
    pairs = ((ids_hbm, ids_ref), (outcome_hbm, outcome_ref), (weight_hbm, weight_ref), (rep_hbm, rep_ref))
    loads = [pltpu.make_async_copy(a, b, in_sem.at[i]) for i, (a, b) in enumerate(pairs)]
    for load in loads:
        load.start()
    rows, width = rep_ref.shape
    earlier = ones_where(iota((rows, rows), 0) < iota((rows, rows), 1))
    loads[0].wait()
    ids = ids_ref[...]
    hot = iota((arms, rows), 0) == ids
    hot_half = ones_where(hot)
    counts = mm(hot_half, earlier)
    rank = jnp.sum(jnp.where(hot, counts, 0.0), axis=0, keepdims=True).astype(I32)
    slot = ids * SLOT + rank
    row8 = iota((8, rows), 0)
    aux_ref[...] = jnp.where(row8 == 0, slot, jnp.where(row8 == 1, rank, ids))
    lane = iota((width, rows), 0)
    loads[1].wait()
    loads[2].wait()
    outcome = outcome_ref[...].astype(F32).reshape(1, rows)
    weight = weight_ref[...].astype(F32).reshape(1, rows)
    side_t = jnp.where(lane == rank, outcome, 0.0) + jnp.where(lane == rank + SLOT, weight, 0.0)
    side = mm(hot_half, side_t.astype(BF16), NT).astype(BF16)
    loads[3].wait()
    rep = rep_ref[...]
    stores = []
    part = arms * SLOT // PARTS
    for i in range(PARTS):
        place = ones_where(iota((part, rows), 0) + i * part == slot)
        cut = pl.ds(i * part, part)
        slots_ref[cut, :] = mm(place, rep).astype(BF16)
        few = part // SLOT
        slots_ref.reshape(arms, SLOT, width)[i * few : (i + 1) * few, SIDE, :] = side[i * few : (i + 1) * few]
        stores.append(pltpu.make_async_copy(slots_ref.at[cut], slots_hbm.at[cut], out_sem.at[i]))
        stores[-1].start()
    for store in stores:
        store.wait()


def side_of(slots, arms):
    return mm(pick_side(arms), slots)


def compact_kernel(arms, packed, slots_ref, send_ref, pos_ref, side_ref):
    total, width = arms * SLOT, slots_ref.shape[2]
    side = slots_ref[:, SIDE, :].astype(F32)
    slots = slots_ref[...].reshape(total, width)
    side_ref[...] = side.astype(BF16)
    lane8 = iota((8, width), 1)
    weight_lanes = ones_where((lane8 >= SLOT) & (lane8 < 2 * SLOT))
    counts = mm(weight_lanes, ones_where(side > 0.0), NT).astype(BF16)
    source, owner = iota((arms, total), 0), iota((arms, total), 1) // SLOT
    start = mm(counts, ones_where(source < owner))
    count = mm(counts, ones_where(source == owner))
    depth = iota((8, total), 1) % SLOT
    pos = jnp.where(depth < count.astype(I32), start.astype(I32) + depth, 2 * packed)
    pos_ref[...] = pos
    half = packed // 2
    for h in range(2):
        gather = ones_where(iota((half, total), 0) + h * half == pos[0:1])
        rows = mm(gather, slots).astype(BF16)
        for d in range(h, send_ref.shape[0], 2):
            send_ref[d] = rows


def prepare_kernel(arms, packed, given_ref, pos_ref, side_ref):
    total, width = arms * SLOT, given_ref.shape[1]
    side = given_ref[...]
    gather = ones_where(iota((packed, total), 0) == pos_ref[0:1])
    same = iota((arms, total), 0) == iota((arms, total), 1) // SLOT
    lane, place = iota((width, total), 0), iota((width, total), 1) % SLOT
    target = mm(side, ones_where(lane == place))
    weight = mm(side, ones_where(lane == place + SLOT))
    target = jnp.sum(jnp.where(same, target, 0.0), axis=0, keepdims=True)
    weight = jnp.sum(jnp.where(same, weight, 0.0), axis=0, keepdims=True)
    both = jnp.where(iota((8, total), 0) == 0, target, weight)
    side_ref[...] = mm(both.astype(BF16), gather, NT)


def unit(pre, head):
    sig = jax.nn.sigmoid(pre)
    return pre * sig, head * sig * (1.0 + pre * (1.0 - sig))


def forward_kernel(
    x_ref, near_ref, far_ref, bh_ref, far_bh_ref, msg_hbm,
    msg_ref, out_sem,
):
    blocks, rows, width = x_ref.shape
    head, far_head = bh_ref[1:2], far_bh_ref[1:2]
    pre = sum(mm(x_ref[j], near_ref[j]) for j in range(blocks)) + bh_ref[0:1]
    act, g = unit(pre, head)
    g = g.astype(BF16)
    pre = sum(mm(x_ref[j], far_ref[j]) for j in range(blocks)) + far_bh_ref[0:1]
    far_act, far_g = unit(pre, far_head)
    far_g = far_g.astype(BF16)
    stores = []
    share = act * head + far_act * far_head
    cut = min(LANES, width)
    share = sum(share[:, i : i + cut] for i in range(0, width, cut))
    share = jnp.sum(jnp.transpose(share), axis=0, keepdims=True)
    high = share.astype(BF16).astype(F32)
    row = iota((EXTRA, rows), 0)
    extra = jnp.where(row == 0, high, jnp.where(row == 1, share - high, 0.0)).astype(BF16)
    for j in range(blocks):
        part = mm(g, near_ref[j], NT) + mm(far_g, far_ref[j], NT)
        msg_ref[j, pl.ds(0, rows), :] = part.astype(BF16)
        msg_ref[j, pl.ds(rows, EXTRA), pl.ds(0, rows)] = extra
        stores.append(pltpu.make_async_copy(msg_ref.at[j], msg_hbm.at[j], out_sem.at[j]))
        stores[-1].start()
    for store in stores:
        store.wait()


def back_kernel(arms, bias_ref, got_ref, side_ref, pos_ref, slots_hbm, resid_ref, slots_ref, sem):
    blocks, rows, width = got_ref.shape
    rows = rows - EXTRA
    total = arms * SLOT
    preds, grads = [], []
    for half in range(2):
        extra = sum(got_ref[j, pl.ds(rows, EXTRA), pl.ds(0, rows)].astype(F32) for j in range(half, blocks, 2))
        preds.append(extra[0:1] + extra[1:2])
        grads.append(sum(got_ref[j, pl.ds(0, rows), :].astype(F32) for j in range(half, blocks, 2)))
    pred = jnp.concatenate(preds, axis=1) + bias_ref[0]
    resid = side_ref[1:2] * (pred - side_ref[0:1])
    resid_ref[...] = jnp.broadcast_to(resid, resid_ref.shape)
    grad = (jnp.concatenate(grads, axis=0) * column(resid)[:, 0:1]).astype(BF16)
    pred = jnp.broadcast_to(pred, (8, 2 * rows)).astype(BF16)
    stores = []
    part = total // PARTS
    for i in range(PARTS):
        cut = pl.ds(i * part, part)
        gather = ones_where(iota((2 * rows, part), 0) == pos_ref[0:1, i * part : (i + 1) * part])
        pred_slot = mm(pred, gather)[0:1]
        row, slot = iota((part, part), 0), iota((part, part), 1)
        spread = jnp.where((row % SLOT == SIDE) & (row // SLOT == slot // SLOT), pred_slot, 0.0).astype(BF16)
        lane = ones_where(iota((width, part), 0) == iota((width, part), 1) % SLOT)
        slots_ref[cut, :] = (mm(gather, grad, TN) + mm(spread, lane, NT)).astype(BF16)
        stores.append(pltpu.make_async_copy(slots_ref.at[cut], slots_hbm.at[cut], sem.at[i]))
        stores[-1].start()
    for store in stores:
        store.wait()


def unpack_kernel(arms, slots_ref, aux_ref, grad_ref, pred_ref):
    total, width = slots_ref.shape
    rows = aux_ref.shape[1]
    slots = slots_ref[...]
    place = ones_where(iota((total, rows), 0) == aux_ref[0:1])
    grad_ref[...] = mm(place, slots, TN).astype(BF16)
    pred_side = slots_ref.reshape(arms, SLOT, width)[:, SIDE, :]
    by_arm = mm(pred_side, ones_where(iota((width, rows), 0) == aux_ref[1:2]))
    hot = iota((arms, rows), 0) == aux_ref[2:3]
    pred = jnp.sum(jnp.where(hot, by_arm, 0.0), axis=0, keepdims=True)
    pred_ref[...] = pred.reshape(rows).astype(BF16)


def grads_kernel(core_ref, x_ref, far_x_ref, near_ref, bh_ref, resid_ref, matrix_ref, bias_ref, head_ref, scalar_ref):
    first = core_ref[0] == 0
    blocks, half, _ = x_ref.shape
    low, high = resid_ref[0:1, 0:half], resid_ref[0:1, half : 2 * half]
    scalar_ref[0] = jnp.sum(resid_ref[0:1])
    mine = column(jnp.where(first, low, high))[:, 0:1]
    other = column(jnp.where(first, high, low))[:, 0:1]
    pre_half, bias, head = [], 0.0, 0.0
    for rows_ref, resid in ((x_ref, mine), (far_x_ref, other)):
        pre = sum(mm(rows_ref[j], near_ref[j]) for j in range(blocks)) + bh_ref[0:1]
        act, g = unit(pre, bh_ref[1:2])
        pre_grad = g * resid
        bias += jnp.sum(pre_grad, axis=0, keepdims=True)
        head += jnp.sum(act * resid, axis=0, keepdims=True)
        pre_half.append(pre_grad.astype(BF16))
    bias_ref[...] = bias
    head_ref[...] = head
    for j in range(blocks):
        matrix_ref[j] = mm(x_ref[j], pre_half[0], TN) + mm(far_x_ref[j], pre_half[1], TN)


def body(rep, arm_ids, outcome, weight, w_hidden, b_hidden, w_head, b_head):
    arms = lax.axis_size("dp")
    tower = lax.axis_size("tower")
    rows, width = rep.shape
    packed = 2 * rows
    total = arms * SLOT
    hidden = w_hidden.shape[2]
    core = (lax.axis_index("tower") % 2).astype(I32).reshape(1)

    def swap(value):
        return lax.ppermute(value, "tower", [(i, i ^ 1) for i in range(tower)])

    def exchange(slots):
        cut = slots.reshape(arms, SLOT, width)
        return lax.all_to_all(cut, "dp", split_axis=0, concat_axis=0, tiled=True).reshape(total, width)

    def spread(blocks):
        return lax.all_to_all(blocks, "tower", split_axis=0, concat_axis=0, tiled=True)

    slots, aux = call(
        functools.partial(pack_kernel, arms),
        (sds((total, width), BF16), sds((8, rows), I32)),
        ins=[HBM] * 4,
        outs=[HBM, VMEM],
        scratch=[
            VMEM((1, rows), I32), VMEM((rows,), BF16), VMEM((rows,), BF16), VMEM((rows, width), BF16),
            VMEM((total, width), BF16), DMA((4,)), DMA((PARTS,)),
        ],
        flops=2 * total * rows * width,
    )(arm_ids.reshape(1, rows), outcome, weight, rep)
    matrix = w_hidden.reshape(tower, width, hidden)
    both = jnp.concatenate([b_hidden, w_head], axis=0)
    far_matrix, far_both = swap(matrix), swap(both)
    arrived = exchange(slots)
    arrived, far_both = lax.optimization_barrier((arrived, far_both))
    send, pos, given = call(
        functools.partial(compact_kernel, arms, packed),
        (sds((tower, rows, width), BF16), sds((8, total), I32), sds((arms, width), BF16)),
        flops=2 * total * packed * width,
    )(arrived.reshape(arms, SLOT, width))
    send, far_matrix = lax.optimization_barrier((send, far_matrix))
    inputs = spread(send)
    (msg,) = call(
        forward_kernel,
        (sds((tower, rows + EXTRA, width), BF16),),
        ins=[VMEM] * 5,
        outs=[HBM],
        scratch=[
            VMEM((tower, rows + EXTRA, width), BF16), DMA((tower,)),
        ],
        flops=8 * rows * tower * width * hidden,
    )(inputs, matrix, far_matrix, both, far_both)
    got = spread(msg)
    msg, later, pos, given = lax.optimization_barrier((msg, inputs, pos, given))
    far_inputs = swap(later)
    (side,) = call(
        functools.partial(prepare_kernel, arms, packed),
        (sds((8, packed), F32),),
        flops=4 * total * packed * arms,
    )(given, pos)
    back_slots, resid = call(
        functools.partial(back_kernel, arms),
        (sds((total, width), BF16), sds((8, packed), F32)),
        ins=[SMEM, VMEM, VMEM, VMEM],
        outs=[HBM, VMEM],
        scratch=[VMEM((total, width), BF16), DMA((PARTS,))],
        flops=2 * total * packed * width,
    )(b_head, got, side, pos)
    returned = exchange(back_slots)
    grad_matrix, grad_bias, grad_vector, grad_scalar = call(
        grads_kernel,
        (
            sds((tower, width, hidden), F32),
            sds((1, hidden), F32),
            sds((1, hidden), F32),
            sds((1,), F32),
        ),
        ins=[SMEM] + [VMEM] * 5,
        outs=[VMEM, VMEM, VMEM, SMEM],
        flops=4 * packed * tower * width * hidden,
        nbytes=5 * 2**20,
    )(core, inputs, far_inputs, matrix, both, resid)
    grad_rep, predicted = call(
        functools.partial(unpack_kernel, arms),
        (sds((rows, width), BF16), sds((rows,), BF16)),
        flops=2 * total * rows * width,
    )(returned, aux)
    return (
        grad_matrix.reshape(1, tower * width, hidden),
        grad_bias,
        grad_vector,
        grad_scalar,
        grad_rep,
        predicted,
    )


def solution(mesh):
    return jax.shard_map(
        body,
        mesh=mesh,
        in_specs=(
            P("dp", "tower"),
            P("dp"),
            P("dp"),
            P("dp"),
            P("dp", None, "tower"),
            P("dp", "tower"),
            P("dp", "tower"),
            P("dp"),
        ),
        out_specs=(
            P("dp", None, "tower"),
            P("dp", "tower"),
            P("dp", "tower"),
            P("dp"),
            P("dp", "tower"),
            P("dp"),
        ),
        check_vma=False,
    )
```
